32 devices in a mesh: pairs: 8 (over z, y), pw: 4 (over x, core).
Axes of the slice: x: 2, y: 2, z: 4, core: 2. Of those that a mesh axis runs over, the one named last changes fastest.
Arguments:
- orbitals: bfloat16 [16, 32, 16384], P(None, 'pairs', 'pw'), may hold values from -6 to 6
- vectors: bfloat16 [16, 64, 256], P(None, 'pairs'), may hold values from -6 to 6
- screened: bfloat16 [16, 2048, 2048], P('pairs', 'pw'), may hold values from -0.00018310547 to 0.00018310547
- pair_list: int32 [16, 2], replicated, may hold values from 0 to 15
- band_order: int32 [32], replicated, may hold values from 0 to 31, each once
Outputs:
- applied: float32 [16, 64, 256], P('pairs', 'pw')
The draws below stay inside these ranges and needn't reach their ends.
All inputs are finite; a program needn't handle non-finite values.
Results may differ from the reference program's by a relative error of at most 0.013.
Values may be sent and summed in bfloat16 or wider, within the bound.
No kernel may reach another device: no remote copies, remote signals or barrier semaphores. Data moves between devices by JAX's collectives and lax.ppermute only.
A program may use at most 128 MiB of HBM per device.

```python
import math
import jax
import jax.numpy as jnp
from jax import lax

NV = 16
NG = 16384
NPW = 2048
NVEC = 64
NB = 32
NT = 256
NK = 16
NPAIRS_ALL = 16


def with_ends(drawn, own_key, low, largest):
    longest = drawn.shape.index(max(drawn.shape))
    spots = []
    for shift in (0, 1):
        where = [jax.random.randint(jax.random.fold_in(own_key, axis), (), 0, length) for axis, length in enumerate(drawn.shape)]
        where[longest] = (where[longest] + shift) % drawn.shape[longest]
        spots.append(tuple(where))
    return drawn.at[spots[0]].set(low).at[spots[1]].set(largest)


def steps_of(rng, extent, pieces, low, high):
    def one(dim, blocks):
        steps = jax.random.uniform(jax.random.fold_in(jax.random.fold_in(rng, 6), dim), (blocks,), jnp.float32, low / len(pieces), high / len(pieces))
        return jnp.repeat(jnp.exp(steps), extent[dim] // blocks).reshape((-1,) + (1,) * (len(extent) - dim - 1))

    loudness = one(*pieces[0])
    for cut in pieces[1:]:
        loudness = loudness * one(*cut)
    return loudness


def normal_values(stream_key, extent, scale, most, shards=(), kind=jnp.bfloat16):
    array = jax.random.normal(stream_key, extent, jnp.float32) * scale
    if len(shards) > 0:
        array = steps_of(stream_key, extent, shards, -0.22, 0.18) * array
    return jnp.clip(array, min=-most, max=most).astype(kind)


def setup_inputs(seed: int = 0) -> dict:
    keys = jax.random.split(jax.random.key(seed), 6)
    orbitals = normal_values(keys[0], (NK, NB, NG), 1.0, 6.0, ((1, 8), (2, 4)))
    vectors = normal_values(keys[1], (NK, NVEC, NT), 1.0, 6.0, ((1, 8),))
    screened = normal_values(keys[2], (NPAIRS_ALL, NPW, NPW), (NPW * NPW * NT) ** -0.5, 0.00018310547, ((0, 8), (1, 4)))
    pair_list = with_ends(jax.random.randint(keys[3], (NPAIRS_ALL, 2), 0, NK), jax.random.fold_in(keys[3], 1), 0, NK - 1).astype(jnp.int32)
    band_order = jax.random.permutation(keys[4], NB).astype(jnp.int32)
    return {"orbitals": orbitals, "vectors": vectors, "screened": screened, "pair_list": pair_list, "band_order": band_order}


def reference(orbitals, vectors, screened, pair_list, band_order):
    picker = (band_order[:, None] == jnp.arange(NB, dtype=jnp.int32)[None, :]).astype(jnp.float32)
    band_psi = jnp.einsum('sb,ksr->kbr', picker, orbitals.astype(jnp.float32)).astype(jnp.bfloat16)
    grid_rows = jnp.arange(NG, dtype=jnp.int32)
    wave_cols = jnp.arange(NPW, dtype=jnp.int32)
    phase_index = (2 * grid_rows + 1)[:, None] * wave_cols[None, :] % (4 * NG)
    cos_table = (jnp.cos(phase_index.astype(jnp.float32) * (math.pi / (2 * NG))) * math.sqrt(2.0 / NG)).astype(jnp.bfloat16)

    def transform(single):
        pair_prod = (single[:NV][:, None, :].astype(jnp.float32) * single[NV:][None, :, :].astype(jnp.float32)).astype(jnp.bfloat16)
        pair_prod = pair_prod.reshape(NT, NG)
        return jnp.dot(pair_prod, cos_table, preferred_element_type=jnp.float32).astype(jnp.bfloat16)
    rho_all = lax.map(transform, band_psi)

    def per_pair(index):
        first_k = pair_list[index, 0]
        second_k = pair_list[index, 1]
        first_rho = rho_all[first_k]
        second_rho = rho_all[second_k]
        screened_rho = jnp.dot(second_rho, screened[index].T, preferred_element_type=jnp.float32).astype(jnp.bfloat16)
        left_proj = jnp.dot(vectors[second_k], screened_rho, preferred_element_type=jnp.float32).astype(jnp.bfloat16)
        right_proj = jnp.dot(vectors[first_k], first_rho, preferred_element_type=jnp.float32).astype(jnp.bfloat16)
        forward = jnp.dot(left_proj, first_rho.T, preferred_element_type=jnp.float32)
        backward = jnp.dot(right_proj, screened_rho.T, preferred_element_type=jnp.float32)
        return (forward, backward)
    forward_all, backward_all = lax.map(per_pair, jnp.arange(NPAIRS_ALL, dtype=jnp.int32))
    applied = jnp.zeros((NK, NVEC, NT), jnp.float32)
    applied = applied.at[pair_list[:, 0]].add(forward_all)
    applied = applied.at[pair_list[:, 1]].add(backward_all)
    return applied
```

```python
import functools
import math

import jax
import jax.numpy as jnp
import numpy as np
from jax import lax
from jax.experimental import pallas as pl
from jax.experimental.pallas import tpu as pltpu
from jax.sharding import PartitionSpec as P

NV = 16
NC = 16
FINE = 64
BF16 = jnp.bfloat16
F32 = jnp.float32


def phase_tables(points, waves, halves, columns):
    width = waves // columns
    sets = []
    for j in range(halves):
        own = np.concatenate(
            [np.arange(c * width, (c + 1) * width) for c in range(j, columns, halves)]
        )
        sets.append(np.concatenate([own[0::2], own[1::2]]))
    sets = np.stack(sets)[:, None, :].astype(np.int64)
    period = 4 * points
    scale = math.sqrt(2.0 / points)
    coarse = (2 * FINE * np.arange(points // FINE)[None, :, None] * sets) % period
    fine = ((2 * np.arange(FINE) + 1)[None, :, None] * sets) % period
    turn = math.pi / (2 * points)
    return (
        (np.cos(coarse * turn) * scale).astype(np.float32),
        (np.sin(coarse * turn) * scale).astype(np.float32),
        np.cos(fine * turn).astype(np.float32),
        np.sin(fine * turn).astype(np.float32),
    )


def one_hot_matrix(size, target):
    rows = lax.broadcasted_iota(jnp.int32, (size, size), 0)
    cols = lax.broadcasted_iota(jnp.int32, (size, size), 1)
    return jnp.where(target(rows) == cols, 1.0, 0.0).astype(BF16)


def interleave(size):
    half = size // 2
    return one_hot_matrix(size, lambda r: jnp.where(r < half, 2 * r, 2 * (r - half) + 1))


def dot(a, b):
    return jnp.dot(a, b, preferred_element_type=F32)


def dot_nt(a, b):
    return lax.dot_general(a, b, (((1,), (1,)), ((), ())), preferred_element_type=F32)


def transform_kernel(
    place, base, mirror, ca, sa, cb, sb, vec, rho, p_first, p_msg, sums, diffs, table, acc
):
    step = pl.program_id(0)
    block = base.shape[-1]
    waves = table.shape[1]
    half = waves // 2
    flip = one_hot_matrix(256, lambda r: 255 - r)

    @pl.when(step == 0)
    def _():
        acc[...] = jnp.zeros_like(acc)

    for a in range(block // FINE):
        table[a * FINE : (a + 1) * FINE, :] = (
            ca[0, a : a + 1, :] * cb[0] - sa[0, a : a + 1, :] * sb[0]
        ).astype(BF16)
    bands = base.shape[3]
    for slot in range(2):
        far = mirror[0, 0, slot]
        back = jnp.concatenate(
            [
                dot(far[:, block - 256 * (i + 1) : block - 256 * i], flip)
                for i in range(block // 256)
            ],
            axis=1,
        )
        near = base[0, 0, slot].astype(F32)
        for v in range(NV):
            here = near[v : v + 1] * near[NV:bands]
            there = back[v : v + 1] * back[NV:bands]
            row = slot * NV * NC + v * NC
            sums[row : row + NC, :] = (here + there).astype(BF16)
            diffs[row : row + NC, :] = (here - there).astype(BF16)
    acc[:, :half] += dot(sums[...], table[:, :half])
    acc[:, half:] += dot(diffs[...], table[:, half:])

    @pl.when(step == pl.num_programs(0) - 1)
    def _():
        order = interleave(256)
        x = place[1]
        width = p_first.shape[1]
        products = NV * NC
        for slot in range(2):
            done = acc[slot * products : (slot + 1) * products, :].astype(BF16)
            rho[slot] = done
            proj = dot(vec[slot], done).astype(BF16)
            natural = jnp.concatenate(
                [
                    dot(
                        jnp.concatenate(
                            [proj[:, 128 * i : 128 * (i + 1)], proj[:, half + 128 * i : half + 128 * (i + 1)]],
                            axis=1,
                        ),
                        order,
                    ).astype(BF16)
                    for i in range(waves // 256)
                ],
                axis=1,
            )
            if slot == 1:
                p_msg[:, width:] = natural
            else:
                first, second = natural[:, :width], natural[:, width:]
                p_first[...] = jnp.where(x == 0, first, second)
                p_msg[:, :width] = jnp.where(x == 0, second, first)


def screen_kernel(place, *refs, shifts):
    j, x = place[0], place[1]
    p_first, p_msg, p_far = refs[:3]
    near = refs[3 : 3 + shifts - 1]
    far = refs[2 + shifts : 1 + 2 * shifts]
    screened = refs[1 + 2 * shifts]
    left_own, left_msg, q_own = refs[2 + 2 * shifts : 5 + 2 * shifts]
    q_msgs = refs[5 + 2 * shifts :]
    width = p_first.shape[1]
    for rel in range(2):
        pair = x if rel == 0 else 1 - x
        first = p_first[...] if rel == 0 else p_far[:, :width]
        total = None
        for s in range(shifts):
            if s == 0:
                source = p_msg if rel == 0 else p_far
                offset = width
            else:
                source = near[s - 1] if rel == 0 else far[s - 1]
                offset = 0
            for c in range(2):
                start = pl.multiple_of((c * shifts + (j ^ s)) * width, width)
                block = screened[pair, :, pl.ds(start, width)]
                piece = source[:, offset + c * width : offset + (c + 1) * width]
                term = dot_nt(piece, block)
                total = term if total is None else total + term
                back = dot(first, block)
                if s == 0:
                    q_own[rel, :, c * width : (c + 1) * width] = back
                else:
                    q_msgs[s - 1][rel, :, c * width : (c + 1) * width] = back.astype(BF16)
        if rel == 0:
            left_own[...] = total.astype(BF16)
        else:
            left_msg[...] = total.astype(BF16)


def apply_kernel(place, left_own, left_far, q_mine, q_far, rho, own, *refs):
    j, x = place[0], place[1]
    msgs, scratch = refs[:-1], refs[-1]
    shifts = len(msgs) + 1
    waves = rho.shape[2]
    half = waves // 2
    order = interleave(256)
    mine, other = left_own[...], left_far[...]
    first = jnp.concatenate([jnp.where(x == 0, mine, other), jnp.where(x == 0, other, mine)], axis=1)
    second = (q_mine[...] + q_far[...].astype(F32)).astype(BF16)
    for slot, weight in enumerate((first, second)):
        parts = [
            dot_nt(weight[:, 256 * i : 256 * (i + 1)], order).astype(BF16)
            for i in range(waves // 256)
        ]
        sorted_weight = jnp.concatenate([p[:, :128] for p in parts] + [p[:, 128:] for p in parts], axis=1)
        scratch[slot] = dot_nt(sorted_weight, rho[slot]).reshape(scratch.shape[1:])
    for s in range(shifts):
        for c in range(2):
            for slot in range(2):
                value = scratch[slot, c * shifts + (j ^ s)]
                if s == 0:
                    own[slot, c] = value
                else:
                    msgs[s - 1][slot, c] = value.astype(BF16)


def local(orbitals, vectors, screened, pair_list, band_order):
    groups = lax.axis_size("pairs")
    columns = lax.axis_size("pw")
    pairs_here = screened.shape[0]
    halves = columns // pairs_here
    both = ("pairs", "pw")
    g = lax.axis_index("pairs")
    w = lax.axis_index("pw")
    x, j = w // halves, w % halves
    place = jnp.stack([j, x]).astype(jnp.int32)
    k_count, band_here, chunk = orbitals.shape
    points = chunk * columns
    waves = screened.shape[2]
    width = waves // columns
    own_waves = width * pairs_here
    transitions = vectors.shape[2]
    vec_count = vectors.shape[1] * groups
    vec_part = vectors.shape[1] // pairs_here
    bands = band_here * groups
    members = [
        [gg * columns + xx * halves + jj for gg in range(groups) for xx in range(pairs_here)]
        for jj in range(halves)
    ]

    def exchange(value):
        return lax.all_to_all(value, both, 0, 0, tiled=True, axis_index_groups=members)

    def shift(value, s):
        return lax.ppermute(value, "pw", [(i, i ^ s) for i in range(columns)])

    vec_mine = lax.dynamic_slice_in_dim(vectors, x * vec_part, vec_part, 1)
    stored = jnp.concatenate([orbitals, vec_mine], axis=2)
    sent = jnp.take(stored, pair_list.reshape(-1), axis=0, mode="clip")
    sent = sent.reshape(groups * pairs_here, 2, band_here, chunk + transitions)
    got = exchange(sent).reshape(groups, pairs_here, 2, band_here, chunk + transitions)
    vec = got[..., chunk:].transpose(2, 0, 1, 3, 4).reshape(2, vec_count, transitions)
    picker = (band_order[:, None] == jnp.arange(bands, dtype=jnp.int32)[None, :]).astype(BF16)
    psi = jnp.einsum(
        "gbn,gxlbr->xlnr",
        picker.reshape(groups, band_here, bands),
        got[..., :chunk],
        preferred_element_type=F32,
    ).astype(BF16)
    parts = [psi] + [shift(psi, s) for s in range(1, halves)]
    count = halves // 2
    base = jnp.stack([parts[s] for s in range(count)])
    mirror = jnp.stack([parts[s ^ (halves - 1)] for s in range(count)])

    block = min(1024, chunk)
    per_chunk = chunk // block
    steps = count * pairs_here * per_chunk
    rows = block // FINE
    tables = [jnp.asarray(t) for t in phase_tables(points, waves, halves, columns)]

    def parse(t):
        return t // (pairs_here * per_chunk), t // per_chunk % pairs_here, t % per_chunk

    def base_map(t, place):
        s, c, b = parse(t)
        return s, c, 0, 0, b

    def mirror_map(t, place):
        s, c, b = parse(t)
        return s, pairs_here - 1 - c, 0, 0, per_chunk - 1 - b

    def coarse_map(t, place):
        s, c, b = parse(t)
        return place[0], (c * halves + (place[0] ^ s)) * per_chunk + b, 0

    def fixed(*shape):
        return pl.BlockSpec(shape, lambda t, place: (0,) * len(shape))

    products = NV * NC
    rho, p_first, p_msg = pl.pallas_call(
        transform_kernel,
        grid_spec=pltpu.PrefetchScalarGridSpec(
            num_scalar_prefetch=1,
            grid=(steps,),
            in_specs=[
                pl.BlockSpec((1, 1, 2, bands, block), base_map),
                pl.BlockSpec((1, 1, 2, bands, block), mirror_map),
                pl.BlockSpec((1, rows, own_waves), coarse_map),
                pl.BlockSpec((1, rows, own_waves), coarse_map),
                pl.BlockSpec((1, FINE, own_waves), lambda t, place: (place[0], 0, 0)),
                pl.BlockSpec((1, FINE, own_waves), lambda t, place: (place[0], 0, 0)),
                fixed(2, vec_count, transitions),
            ],
            out_specs=[
                fixed(2, products, own_waves),
                fixed(vec_count, width),
                fixed(vec_count, width + own_waves),
            ],
            scratch_shapes=[
                pltpu.VMEM((2 * products, block), BF16),
                pltpu.VMEM((2 * products, block), BF16),
                pltpu.VMEM((block, own_waves), BF16),
                pltpu.VMEM((2 * products, own_waves), F32),
            ],
        ),
        out_shape=[
            jax.ShapeDtypeStruct((2, products, own_waves), BF16),
            jax.ShapeDtypeStruct((vec_count, width), BF16),
            jax.ShapeDtypeStruct((vec_count, width + own_waves), BF16),
        ],
        compiler_params=pltpu.CompilerParams(vmem_limit_bytes=40 * 2**20),
        name="transform",
    )(place, base, mirror, *tables, vec)

    p_far = shift(p_msg, halves)
    near = [shift(p_msg[:, width:], s) for s in range(1, halves)]
    far = [shift(p_far[:, width:], s) for s in range(1, halves)]
    smem = pl.BlockSpec(memory_space=pltpu.SMEM)
    vmem = pl.BlockSpec(memory_space=pltpu.VMEM)
    left_own, left_msg, q_own, *q_msgs = pl.pallas_call(
        functools.partial(screen_kernel, shifts=halves),
        in_specs=[smem] + [vmem] * (3 + 2 * (halves - 1) + 1),
        out_specs=[vmem] * (3 + halves - 1),
        out_shape=[
            jax.ShapeDtypeStruct((vec_count, width), BF16),
            jax.ShapeDtypeStruct((vec_count, width), BF16),
            jax.ShapeDtypeStruct((2, vec_count, own_waves), F32),
        ]
        + [jax.ShapeDtypeStruct((2, vec_count, own_waves), BF16)] * (halves - 1),
        compiler_params=pltpu.CompilerParams(vmem_limit_bytes=24 * 2**20),
        name="screen",
    )(place, p_first, p_msg, p_far, *near, *far, screened)
    left_far = shift(left_msg, halves)
    for s in range(1, halves):
        q_own = q_own + shift(q_msgs[s - 1], s).astype(F32)
    q_far = shift(q_own[1].astype(BF16), halves)

    vec_rows = vec_count // columns
    out_own, *out_msgs = pl.pallas_call(
        apply_kernel,
        in_specs=[smem] + [vmem] * 5,
        out_specs=[vmem] * halves,
        out_shape=[jax.ShapeDtypeStruct((2, pairs_here, vec_rows, transitions), F32)]
        + [jax.ShapeDtypeStruct((2, pairs_here, vec_rows, transitions), BF16)] * (halves - 1),
        scratch_shapes=[pltpu.VMEM((2, columns, vec_rows, transitions), F32)],
        compiler_params=pltpu.CompilerParams(vmem_limit_bytes=24 * 2**20),
        name="apply",
    )(place, left_own, left_far, q_own[0], q_far, rho)
    for s in range(1, halves):
        out_own = out_own + shift(out_msgs[s - 1], s).astype(F32)
    mine = lax.dynamic_slice_in_dim(pair_list, g * pairs_here + x, 1, 0).reshape(-1)
    k_here = k_count // groups
    owners = jnp.arange(k_count, dtype=jnp.int32).reshape(groups, 1, k_here, 1, 1)
    placed = sum(
        jnp.where(mine[slot] == owners, out_own[slot][None, :, None], 0.0) for slot in range(2)
    ).astype(BF16)
    placed = placed.reshape(groups * pairs_here, k_here, vec_rows, transitions)
    return jnp.sum(exchange(placed).astype(F32), axis=0)


def solution(mesh):
    in_specs = (P(None, "pairs", "pw"), P(None, "pairs", None), P("pairs", "pw", None), P(), P())
    out_specs = P("pairs", "pw", None)
    return jax.shard_map(local, mesh=mesh, in_specs=in_specs, out_specs=out_specs, check_vma=False)
```

```python
import functools
import math

import jax
import jax.numpy as jnp
import numpy as np
from jax import lax
from jax.experimental import pallas as pl
from jax.experimental.pallas import tpu as pltpu
from jax.sharding import PartitionSpec as P

NV = 16
NC = 16
FINE = 64
BF16 = jnp.bfloat16
F32 = jnp.float32


def phase_tables(points, waves, halves, columns):
    width = waves // columns
    sets = []
    for j in range(halves):
        own = np.concatenate(
            [np.arange(c * width, (c + 1) * width) for c in range(j, columns, halves)]
        )
        sets.append(np.concatenate([own[0::2], own[1::2]]))
    sets = np.stack(sets)[:, None, :].astype(np.int64)
    period = 4 * points
    scale = math.sqrt(2.0 / points)
    coarse = (2 * FINE * np.arange(points // FINE)[None, :, None] * sets) % period
    fine = ((2 * np.arange(FINE) + 1)[None, :, None] * sets) % period
    turn = math.pi / (2 * points)
    return (
        (np.cos(coarse * turn) * scale).astype(np.float32),
        (np.sin(coarse * turn) * scale).astype(np.float32),
        np.cos(fine * turn).astype(np.float32),
        np.sin(fine * turn).astype(np.float32),
    )


def one_hot_matrix(size, target):
    rows = lax.broadcasted_iota(jnp.int32, (size, size), 0)
    cols = lax.broadcasted_iota(jnp.int32, (size, size), 1)
    return jnp.where(target(rows) == cols, 1.0, 0.0).astype(BF16)


def interleave(size):
    half = size // 2
    return one_hot_matrix(size, lambda r: jnp.where(r < half, 2 * r, 2 * (r - half) + 1))


def dot(a, b):
    return jnp.dot(a, b, preferred_element_type=F32)


def dot_nt(a, b):
    return lax.dot_general(a, b, (((1,), (1,)), ((), ())), preferred_element_type=F32)


def gather_kernel(requests, place, orbitals, vectors, out, sem):
    count, slots, rows = out.shape[:3]
    chunk = orbitals.shape[2]
    copies = []
    for i in range(count * slots):
        copies.append(
            pltpu.make_async_copy(
                orbitals.at[requests[i]], out.at[i // slots, i % slots, :, pl.ds(0, chunk)], sem.at[i]
            )
        )
    for copy in copies:
        copy.start()
    for i in range(count * slots):
        block = vectors[requests[i]]
        part = jnp.where(place[1] == 0, block[:rows], block[rows:])
        out[i // slots, i % slots, :, chunk:] = part
    for copy in copies:
        copy.wait()


def table_kernel(place, ca, sa, cb, sb, table, *, chunk, halves):
    j = place[0]
    rows = chunk // FINE
    for i in range(table.shape[0] // chunk):
        first = ((i % 2) * halves + (j ^ (i // 2))) * rows

        def step(a, carry):
            start = pl.multiple_of(i * chunk + a * FINE, FINE)
            table[pl.ds(start, FINE), :] = (
                ca[j, pl.ds(first + a, 1), :] * cb[j] - sa[j, pl.ds(first + a, 1), :] * sb[j]
            ).astype(BF16)
            return carry

        lax.fori_loop(0, rows, step, 0, unroll=4)


def transform_kernel(place, *refs, halves, slot):
    parts = refs[:halves]
    table, vec, rho = refs[halves : halves + 3]
    outs = refs[halves + 3 : -3]
    sums, diffs, acc = refs[-3:]
    chunk = parts[0].shape[2]
    block = sums.shape[2]
    waves = table.shape[1]
    half = waves // 2
    flip = one_hot_matrix(256, lambda r: 255 - r)
    per_chunk = chunk // block
    bands = parts[0].shape[1]
    for t in range(table.shape[0] // block):
        s, c, b = t // (2 * per_chunk), t // per_chunk % 2, t % per_chunk
        mirror = parts[s ^ (halves - 1)]
        end = chunk - b * block
        back = jnp.concatenate(
            [
                dot(mirror[1 - c, :, end - 256 * (i + 1) : end - 256 * i], flip)
                for i in range(block // 256)
            ],
            axis=1,
        )
        near = parts[s][c, :, b * block : (b + 1) * block].astype(F32)
        for v in range(NV):
            here = near[v : v + 1] * near[NV:bands]
            there = back[v : v + 1] * back[NV:bands]
            sums[t % 2, v * NC : (v + 1) * NC, :] = (here + there).astype(BF16)
            diffs[t % 2, v * NC : (v + 1) * NC, :] = (here - there).astype(BF16)
        even = dot(sums[t % 2], table[t * block : (t + 1) * block, :half])
        odd = dot(diffs[t % 2], table[t * block : (t + 1) * block, half:])
        if t == 0:
            acc[:, :half] = even
            acc[:, half:] = odd
        else:
            acc[:, :half] += even
            acc[:, half:] += odd
    done = acc[...].astype(BF16)
    rho[...] = done
    order = interleave(256)
    proj = dot(vec[...], done).astype(BF16)
    natural = jnp.concatenate(
        [
            dot(
                jnp.concatenate(
                    [proj[:, 128 * i : 128 * (i + 1)], proj[:, half + 128 * i : half + 128 * (i + 1)]],
                    axis=1,
                ),
                order,
            ).astype(BF16)
            for i in range(waves // 256)
        ],
        axis=1,
    )
    if slot == 1:
        outs[0][...] = natural
    else:
        x = place[1]
        width = outs[0].shape[1]
        first, second = natural[:, :width], natural[:, width:]
        outs[0][...] = jnp.where(x == 0, first, second)
        outs[1][...] = jnp.where(x == 0, second, first)


def back_kernel(place, p_own, p_far, screened, q_own, *q_msgs):
    j, x = place[0], place[1]
    shifts = len(q_msgs) + 1
    width = p_own.shape[1]
    for rel in range(2):
        pair = x if rel == 0 else 1 - x
        first = p_own[...] if rel == 0 else p_far[...]
        for s in range(shifts):
            for c in range(2):
                start = pl.multiple_of((c * shifts + (j ^ s)) * width, width)
                back = dot(first, screened[pair, :, pl.ds(start, width)])
                if s == 0:
                    q_own[rel, :, c * width : (c + 1) * width] = back
                else:
                    q_msgs[s - 1][rel, :, c * width : (c + 1) * width] = back.astype(BF16)


def left_kernel(place, *refs):
    j, x = place[0], place[1]
    sources, (screened, left_own, left_msg) = refs[:-3], refs[-3:]
    shifts = len(sources) // 2
    width = left_own.shape[1]
    for rel in range(2):
        pair = x if rel == 0 else 1 - x
        total = None
        for s in range(shifts):
            source = sources[rel * shifts + s]
            for c in range(2):
                start = pl.multiple_of((c * shifts + (j ^ s)) * width, width)
                term = dot_nt(
                    source[:, c * width : (c + 1) * width], screened[pair, :, pl.ds(start, width)]
                )
                total = term if total is None else total + term
        (left_msg if rel else left_own)[...] = total.astype(BF16)


def apply_kernel(place, left_own, left_far, q_mine, q_far, rho_first, rho_second, own, *refs):
    j, x = place[0], place[1]
    msgs, scratch = refs[:-1], refs[-1]
    shifts = len(msgs) + 1
    waves = rho_first.shape[1]
    order = interleave(256)
    mine, other = left_own[...], left_far[...]
    first = jnp.concatenate([jnp.where(x == 0, mine, other), jnp.where(x == 0, other, mine)], axis=1)
    second = (q_mine[...] + q_far[...].astype(F32)).astype(BF16)
    for slot, weight in enumerate((first, second)):
        parts = [
            dot_nt(weight[:, 256 * i : 256 * (i + 1)], order).astype(BF16)
            for i in range(waves // 256)
        ]
        sorted_weight = jnp.concatenate([p[:, :128] for p in parts] + [p[:, 128:] for p in parts], axis=1)
        scratch[slot] = dot_nt(sorted_weight, (rho_first, rho_second)[slot][...]).reshape(scratch.shape[1:])
    for s in range(shifts):
        for c in range(2):
            for slot in range(2):
                value = scratch[slot, c * shifts + (j ^ s)]
                if s == 0:
                    own[slot, c] = value
                else:
                    msgs[s - 1][slot, c] = value.astype(BF16)


def local(orbitals, vectors, screened, pair_list, band_order):
    groups = lax.axis_size("pairs")
    columns = lax.axis_size("pw")
    pairs_here = screened.shape[0]
    halves = columns // pairs_here
    both = ("pairs", "pw")
    g = lax.axis_index("pairs")
    w = lax.axis_index("pw")
    x, j = w // halves, w % halves
    place = jnp.stack([j, x]).astype(jnp.int32)
    k_count, band_here, chunk = orbitals.shape
    points = chunk * columns
    waves = screened.shape[2]
    width = waves // columns
    own_waves = width * pairs_here
    transitions = vectors.shape[2]
    vec_count = vectors.shape[1] * groups
    vec_part = vectors.shape[1] // pairs_here
    bands = band_here * groups
    members = [
        [gg * columns + xx * halves + jj for gg in range(groups) for xx in range(pairs_here)]
        for jj in range(halves)
    ]

    def exchange(value):
        return lax.all_to_all(value, both, 0, 0, tiled=True, axis_index_groups=members)

    def shift(value, s):
        return lax.ppermute(value, "pw", [(i, i ^ s) for i in range(columns)])

    def call(kernel, outs, *args, flops=0, scratch=(), limit=4, scalars=1):
        moved = sum(math.prod(v.shape) * v.dtype.itemsize for v in (*args, *outs))
        return pl.pallas_call(
            kernel,
            in_specs=[smem] * scalars + [vmem] * (len(args) - scalars),
            out_specs=[vmem] * len(outs),
            out_shape=list(outs),
            scratch_shapes=list(scratch),
            compiler_params=pltpu.CompilerParams(vmem_limit_bytes=limit * 2**20),
            cost_estimate=pl.CostEstimate(flops=flops, bytes_accessed=moved, transcendentals=0),
        )(*args)

    smem = pl.BlockSpec(memory_space=pltpu.SMEM)
    vmem = pl.BlockSpec(memory_space=pltpu.VMEM)
    like = jax.ShapeDtypeStruct

    slots = 2 * groups * pairs_here
    sent = pl.pallas_call(
        gather_kernel,
        in_specs=[smem, smem, pl.BlockSpec(memory_space=pl.ANY), vmem],
        out_specs=vmem,
        out_shape=like((slots // 2, 2, band_here, chunk + transitions), BF16),
        scratch_shapes=[pltpu.SemaphoreType.DMA((slots,))],
        compiler_params=pltpu.CompilerParams(vmem_limit_bytes=8 * 2**20),
    )(pair_list.reshape(-1), place, orbitals, vectors)
    got = exchange(sent).reshape(groups, pairs_here, 2, band_here, chunk + transitions)
    tables = [jnp.asarray(t) for t in phase_tables(points, waves, halves, columns)]
    (table,) = call(
        functools.partial(table_kernel, chunk=chunk, halves=halves),
        [like((points // 2, own_waves), BF16)],
        place,
        *tables,
        flops=3 * points // 2 * own_waves,
        limit=2,
    )
    vec = got[..., chunk:].transpose(2, 0, 1, 3, 4).reshape(2, vec_count, transitions)
    picker = (band_order[:, None] == jnp.arange(bands, dtype=jnp.int32)[None, :]).astype(BF16)
    psi = jnp.einsum(
        "gbn,gxlbr->lxnr",
        picker.reshape(groups, band_here, bands),
        got[..., :chunk],
        preferred_element_type=F32,
    ).astype(BF16)
    products = NV * NC
    block = min(2048, chunk)

    def transform(slot, outs):
        parts = [psi[slot]] + [shift(psi[slot], s) for s in range(1, halves)]
        return call(
            functools.partial(transform_kernel, halves=halves, slot=slot),
            [like((products, own_waves), BF16)] + outs,
            place,
            *parts,
            table,
            vec[slot],
            flops=products * points * own_waves,
            scratch=[pltpu.VMEM((2, products, block), BF16)] * 2
            + [pltpu.VMEM((products, own_waves), F32)],
            limit=12,
        )

    shape = like((vec_count, width), BF16)
    full = like((vec_count, own_waves), BF16)
    rho_first, p_own, p_msg = transform(0, [shape, shape])
    rho_second, p_second = transform(1, [full])
    p_far = shift(p_msg, halves)
    far = shift(p_second, halves)
    near = [shift(p_second, s) for s in range(1, halves)]
    fars = [shift(far, s) for s in range(1, halves)]
    both_q = like((2, vec_count, own_waves), F32)
    flops = 4 * vec_count * width * waves
    q_own, *q_msgs = call(
        back_kernel,
        [both_q] + [like(both_q.shape, BF16)] * (halves - 1),
        place,
        p_own,
        p_far,
        screened,
        flops=flops,
    )
    for s in range(1, halves):
        q_own = q_own + shift(q_msgs[s - 1], s).astype(F32)
    q_far = shift(q_own[1].astype(BF16), halves)
    left_own, left_msg = call(
        left_kernel, [shape, shape], place, p_second, *near, far, *fars, screened, flops=flops
    )
    left_far = shift(left_msg, halves)

    vec_rows = vec_count // columns
    terms = like((2, pairs_here, vec_rows, transitions), F32)
    out_own, *out_msgs = call(
        apply_kernel,
        [terms] + [like(terms.shape, BF16)] * (halves - 1),
        place,
        left_own,
        left_far,
        q_own[0],
        q_far,
        rho_first,
        rho_second,
        flops=4 * vec_count * products * own_waves,
        scratch=[pltpu.VMEM((2, columns, vec_rows, transitions), F32)],
    )
    for s in range(1, halves):
        out_own = out_own + shift(out_msgs[s - 1], s).astype(F32)
    mine = lax.dynamic_slice_in_dim(pair_list, g * pairs_here + x, 1, 0).reshape(-1)
    k_here = k_count // groups
    owners = jnp.arange(k_count, dtype=jnp.int32).reshape(groups, 1, k_here, 1, 1)
    placed = sum(
        jnp.where(mine[slot] == owners, out_own[slot][None, :, None], 0.0) for slot in range(2)
    ).astype(BF16)
    placed = placed.reshape(groups * pairs_here, k_here, vec_rows, transitions)
    return jnp.sum(exchange(placed).astype(F32), axis=0)


def solution(mesh):
    in_specs = (P(None, "pairs", "pw"), P(None, "pairs", None), P("pairs", "pw", None), P(), P())
    out_specs = P("pairs", "pw", None)
    return jax.shard_map(local, mesh=mesh, in_specs=in_specs, out_specs=out_specs, check_vma=False)
```

```python
import functools
import math

import jax
import jax.numpy as jnp
import numpy as np
from jax import lax
from jax.experimental import pallas as pl
from jax.experimental.pallas import tpu as pltpu
from jax.sharding import PartitionSpec as P

NV = 16
NC = 16
FINE = 64
BF16 = jnp.bfloat16
F32 = jnp.float32


def column_order(size):
    return np.concatenate([np.arange(0, size, 4), np.arange(2, size, 4), np.arange(1, size, 2)])


def phase_tables(points, waves, halves, columns):
    width, chunk = waves // columns, points // columns
    period, turn = 4 * points, math.pi / (2 * points)
    scale = math.sqrt(2.0 / points)
    seeds = []
    for j in range(halves):
        own = np.concatenate(
            [np.arange(c * width, (c + 1) * width) for c in range(j, columns, halves)]
        )
        own = own[column_order(own.size)].astype(np.int64)
        starts = np.concatenate(
            [
                np.arange((c * halves + (j ^ s)) * chunk, (c * halves + (j ^ s) + 1) * chunk, FINE)
                for s in range(halves // 2)
                for c in range(columns // halves)
            ]
        )
        coarse = (2 * starts[:, None] * own) % period * turn
        fine = ((2 * np.arange(FINE) + 1)[:, None] * own) % period * turn
        seeds.append(
            [
                np.concatenate([np.cos(coarse) * scale, np.cos(fine)]),
                np.concatenate([np.sin(coarse) * scale, np.sin(fine)]),
            ]
        )
    return np.array(seeds).astype(np.float32)


def one_hot_matrix(size, target):
    rows = lax.broadcasted_iota(jnp.int32, (size, size), 0)
    cols = lax.broadcasted_iota(jnp.int32, (size, size), 1)
    return jnp.where(target(rows) == cols, 1.0, 0.0).astype(BF16)


def interleave(size):
    part = size // 4
    return one_hot_matrix(
        size,
        lambda r: jnp.where(r < part, 4 * r, jnp.where(r < 2 * part, 4 * r - size + 2, 2 * r - size + 1)),
    )


def pieces(waves, i, size):
    part, quarter = size // 4, waves // 4
    yield i * part, part
    yield quarter + i * part, part
    yield 2 * quarter + 2 * i * part, 2 * part


def place(halves):
    w = lax.axis_index("pw")
    return lax.rem(w, halves), lax.div(w, halves)


def dot(a, b):
    return jnp.dot(a, b, preferred_element_type=F32)


def dot_nt(a, b):
    return lax.dot_general(a, b, (((1,), (1,)), ((), ())), preferred_element_type=F32)


def gather_kernel(requests, orbitals, vectors, out, held, load, store, *, halves):
    count, slots, rows = out.shape[:3]
    chunk = orbitals.shape[2]
    spots = [(i // slots, i % slots) for i in range(count * slots)]
    loads = [
        pltpu.make_async_copy(
            orbitals.at[requests[slot, i]], held.at[i, slot, :, pl.ds(0, chunk)], load.at[i, slot]
        )
        for i, slot in spots
    ]
    for copy in loads:
        copy.start()
    x = place(halves)[1]
    for i, slot in spots:
        block = vectors[requests[slot, i]]
        held[i, slot, :, chunk:] = jnp.where(x == 0, block[:rows], block[rows:])
    stores = []
    for copy, (i, slot) in zip(loads, spots):
        copy.wait()
        if slot == slots - 1:
            stores.append(pltpu.make_async_copy(held.at[i], out.at[i], store.at[i]))
            stores[-1].start()
    for copy in stores:
        copy.wait()


def transform_kernel(*refs, halves, slot):
    parts = refs[:halves]
    seeds, vec = refs[halves : halves + 2]
    refs = refs[halves + 2 :]
    if slot == 1:
        far_screened, rho, natural_out, screened = refs[:4]
        copy = pltpu.make_async_copy(far_screened, screened, refs[-1])
        copy.start()
        refs = refs[:-1]
    else:
        rho, p_own, p_msg = refs[:3]
    evens, odds, table, acc = refs[-4:]
    x = place(halves)[1]
    chunk = parts[0].shape[2]
    block = evens.shape[3]
    waves = acc.shape[1]
    half, quarter = waves // 2, waves // 4
    flip = one_hot_matrix(256, lambda r: 255 - r)
    per_chunk = chunk // block
    bands = parts[0].shape[1]
    coarse = seeds.shape[1] - FINE
    rows = chunk // FINE
    for t in range(halves // 2 * per_chunk):
        s, b = t // per_chunk, t % per_chunk
        now = t % 2
        end = chunk - b * block
        near, back = [], []
        for c in range(2):
            mirror = parts[s ^ (halves - 1)]
            back.append(
                jnp.concatenate(
                    [
                        dot(mirror[1 - c, :, end - 256 * (i + 1) : end - 256 * i], flip)
                        for i in range(block // 256)
                    ],
                    axis=1,
                )
            )
            near.append(parts[s][c, :, b * block : (b + 1) * block].astype(F32))
        for v in range(NV):
            to = slice(v * NC, (v + 1) * NC)
            even = []
            for c in range(2):
                here = near[c][v : v + 1] * near[c][NV:bands]
                there = back[c][v : v + 1] * back[c][NV:bands]
                even.append(here + there)
                odds[now, to, c * block : (c + 1) * block] = (here - there).astype(BF16)
            evens[now, 0, to, :] = (even[0] + even[1]).astype(BF16)
            evens[now, 1, to, :] = (even[0] - even[1]).astype(BF16)
        for c in range(2):
            cols = slice(0, waves) if c == 0 else slice(half, waves)
            cb, sb = seeds[0, coarse:, cols], seeds[1, coarse:, cols]
            for a in range(block // FINE):
                row = (s * 2 + c) * rows + b * (block // FINE) + a
                table[now, c * block + a * FINE : c * block + (a + 1) * FINE, cols] = (
                    seeds[0, row : row + 1, cols] * cb - seeds[1, row : row + 1, cols] * sb
                ).astype(BF16)
        terms = (
            dot(evens[now, 0], table[now, :block, :quarter]),
            dot(evens[now, 1], table[now, :block, quarter:half]),
            dot(odds[now], table[now, :, half:]),
        )
        for cols, term in zip((slice(0, quarter), slice(quarter, half), slice(half, waves)), terms):
            if t == 0:
                acc[:, cols] = term
            else:
                acc[:, cols] += term
    done = acc[...].astype(BF16)
    rho[...] = done
    size = min(512, waves)
    order = interleave(size)
    proj = dot(vec[...], done).astype(BF16)
    natural = jnp.concatenate(
        [
            dot(
                jnp.concatenate([proj[:, o : o + n] for o, n in pieces(waves, i, size)], axis=1),
                order,
            ).astype(BF16)
            for i in range(waves // size)
        ],
        axis=1,
    )
    if slot == 1:
        natural_out[...] = natural
        copy.wait()
    else:
        width = p_own.shape[1]
        first, second = natural[:, :width], natural[:, width:]
        p_own[...] = jnp.where(x == 0, first, second)
        p_msg[...] = jnp.where(x == 0, second, first)


def back_kernel(p_own, p_far, screened, q_keep, q_part, *q_msgs):
    shifts = len(q_msgs) + 1
    j, x = place(shifts)
    width = p_own.shape[1]
    for rel in range(2):
        pair = x if rel == 0 else 1 - x
        first = p_own[...] if rel == 0 else p_far[...]
        for s in range(shifts):
            for c in range(2):
                start = pl.multiple_of((c * shifts + (j ^ s)) * width, width)
                term = dot(first, screened[pair, :, pl.ds(start, width)])
                cols = slice(c * width, (c + 1) * width)
                if s == 0:
                    (q_part if rel else q_keep)[:, cols] = term
                else:
                    q_msgs[s - 1][rel, :, cols] = term.astype(BF16)


def left_kernel(*refs):
    sources, (screened, left_own, left_msg) = refs[:-3], refs[-3:]
    shifts = len(sources) // 2
    j, x = place(shifts)
    width = left_own.shape[1]
    for rel in range(2):
        pair = x if rel == 0 else 1 - x
        total = None
        for s in range(shifts):
            source = sources[rel * shifts + s]
            for c in range(2):
                start = pl.multiple_of((c * shifts + (j ^ s)) * width, width)
                term = dot_nt(
                    source[:, c * width : (c + 1) * width], screened[pair, :, pl.ds(start, width)]
                )
                total = term if total is None else total + term
        (left_msg if rel else left_own)[...] = total.astype(BF16)


def apply_weight(weight, rho, scratch, outs):
    shifts = len(outs)
    j = place(shifts)[0]
    waves = rho.shape[1]
    size = min(512, waves)
    order = interleave(size)
    parts = [
        dot_nt(weight[:, size * i : size * (i + 1)], order).astype(BF16)
        for i in range(waves // size)
    ]
    cuts = (0, size // 4, size // 2, size)
    sorted_weight = jnp.concatenate(
        [p[:, lo:hi] for lo, hi in zip(cuts, cuts[1:]) for p in parts], axis=1
    )
    scratch[...] = dot_nt(sorted_weight, rho[...]).reshape(scratch.shape)
    for s in range(shifts):
        for c in range(2):
            outs[s][c] = scratch[c * shifts + (j ^ s)].astype(outs[s].dtype)


def apply_second_kernel(q_keep, q_far, *refs):
    shifts = (len(refs) - 1) // 2
    received, rho = refs[: shifts - 1], refs[shifts - 1]
    outs, scratch = refs[shifts:-1], refs[-1]
    weight = q_keep[...] + q_far[...].astype(F32)
    for part in received:
        weight = weight + part[0].astype(F32)
    apply_weight(weight.astype(BF16), rho, scratch, outs)


def apply_first_kernel(left_own, left_far, rho, *refs):
    shifts = (len(refs) - 1) // 2
    others, outs, scratch = refs[:shifts], refs[shifts:-1], refs[-1]
    x = place(shifts)[1]
    mine, other = left_own[...], left_far[...]
    weight = jnp.concatenate(
        [jnp.where(x == 0, mine, other), jnp.where(x == 0, other, mine)], axis=1
    )
    apply_weight(weight, rho, scratch, [out.at[0] for out in outs])
    for out, second in zip(outs, others):
        out[1] = second[...]


def send_kernel(pairs, own, *refs, groups, halves):
    received, out = refs[:-1], refs[-1]
    slots, parts = own.shape[:2]
    x = place(halves)[1]
    index = lax.axis_index("pairs") * parts + x
    owned = out.shape[1]
    total = own[...]
    for part in received:
        total = total + part[...].astype(F32)
    for k in range(groups * owned):
        for part in range(parts):
            value = jnp.zeros(own.shape[2:], F32)
            for slot in range(slots):
                value = value + jnp.where(pairs[slot, index] == k, total[slot, part], 0.0)
            out[k // owned * parts + part, k % owned] = value.astype(BF16)


def local(orbitals, vectors, screened, pair_list, band_order):
    groups = lax.axis_size("pairs")
    columns = lax.axis_size("pw")
    pairs_here = screened.shape[0]
    halves = columns // pairs_here
    both = ("pairs", "pw")
    w = lax.axis_index("pw")
    k_count, band_here, chunk = orbitals.shape
    points = chunk * columns
    waves = screened.shape[2]
    width = waves // columns
    own_waves = width * pairs_here
    transitions = vectors.shape[2]
    vec_count = vectors.shape[1] * groups
    vec_part = vectors.shape[1] // pairs_here
    bands = band_here * groups
    members = [
        [gg * columns + xx * halves + jj for gg in range(groups) for xx in range(pairs_here)]
        for jj in range(halves)
    ]

    def exchange(value):
        return lax.all_to_all(value, both, 0, 0, tiled=True, axis_index_groups=members)

    def shift(value, s):
        return lax.ppermute(value, "pw", [(i, i ^ s) for i in range(columns)])

    def call(kernel, outs, *args, flops=0, scratch=(), limit=4, far=0):
        moved = sum(math.prod(v.shape) * v.dtype.itemsize for v in (*args, *outs))
        return pl.pallas_call(
            kernel,
            in_specs=[vmem] * (len(args) - far) + [hbm] * far,
            out_specs=[vmem] * len(outs),
            out_shape=list(outs),
            scratch_shapes=list(scratch),
            compiler_params=pltpu.CompilerParams(vmem_limit_bytes=limit * 2**20),
            cost_estimate=pl.CostEstimate(flops=flops, bytes_accessed=moved, transcendentals=0),
        )(*args)

    smem = pl.BlockSpec(memory_space=pltpu.SMEM)
    vmem = pl.BlockSpec(memory_space=pltpu.VMEM)
    hbm = pl.BlockSpec(memory_space=pltpu.HBM)
    like = jax.ShapeDtypeStruct

    slots = 2 * groups * pairs_here
    sent = pl.pallas_call(
        functools.partial(gather_kernel, halves=halves),
        in_specs=[smem, hbm, vmem],
        out_specs=hbm,
        out_shape=like((slots // 2, 2, band_here, chunk + transitions), BF16),
        scratch_shapes=[
            pltpu.VMEM((slots // 2, 2, band_here, chunk + transitions), BF16),
            pltpu.SemaphoreType.DMA((slots // 2, 2)),
            pltpu.SemaphoreType.DMA((slots // 2,)),
        ],
        compiler_params=pltpu.CompilerParams(vmem_limit_bytes=60 * 2**20),
    )(pair_list.T, orbitals, vectors)
    got = exchange(sent).reshape(groups, pairs_here, 2, band_here, chunk + transitions)
    seeds = lax.dynamic_index_in_dim(
        jnp.asarray(phase_tables(points, waves, halves, columns)), w % halves, keepdims=False
    )
    vec = got[..., chunk:].transpose(2, 0, 1, 3, 4).reshape(2, vec_count, transitions)
    picker = (band_order[:, None] == jnp.arange(bands, dtype=jnp.int32)[None, :]).astype(BF16)
    picker, seeds = lax.optimization_barrier((picker, seeds))
    psi = jnp.einsum(
        "gbn,gxlbr->lxnr",
        picker.reshape(groups, band_here, bands),
        got[..., :chunk],
        preferred_element_type=F32,
    ).astype(BF16)
    products = NV * NC
    block = min(1024, chunk)

    def transform(slot, outs, *far):
        parts = [psi[slot]] + [shift(psi[slot], s) for s in range(1, halves)]
        return call(
            functools.partial(transform_kernel, halves=halves, slot=slot),
            [like((products, own_waves), BF16)] + outs,
            *parts,
            seeds,
            vec[slot],
            *far,
            flops=products * points * own_waves,
            scratch=[
                pltpu.VMEM((2, 2, products, block), BF16),
                pltpu.VMEM((2, products, 2 * block), BF16),
                pltpu.VMEM((2, 2 * block, own_waves), BF16),
                pltpu.VMEM((products, own_waves), F32),
            ]
            + [pltpu.SemaphoreType.DMA] * len(far),
            limit=24,
            far=len(far),
        )

    shape = like((vec_count, width), BF16)
    full = like((vec_count, own_waves), BF16)
    rho_first, p_own, p_msg = transform(0, [shape, shape])
    rho_second, p_second, screened = transform(1, [full, like(screened.shape, BF16)], screened)
    p_far = shift(p_msg, halves)
    p_own, p_second = lax.optimization_barrier((p_own, p_second))
    far = shift(p_second, halves)
    near = [shift(p_second, s) for s in range(1, halves)]
    fars = [shift(far, s) for s in range(1, halves)]
    flops = 4 * vec_count * width * waves
    partial_q = like((vec_count, own_waves), F32)
    q_keep, q_part, *q_msgs = call(
        back_kernel,
        [partial_q] * 2 + [like((2, vec_count, own_waves), BF16)] * (halves - 1),
        p_own,
        p_far,
        screened,
        flops=flops,
    )
    received = [shift(q_msgs[s - 1], s) for s in range(1, halves)]
    q_send = (q_part + sum(v[1].astype(F32) for v in received)).astype(BF16)
    q_far = shift(q_send, halves)
    left_own, left_msg = call(
        left_kernel, [shape, shape], p_second, *near, far, *fars, screened, flops=flops
    )
    left_far = shift(left_msg, halves)

    vec_rows = vec_count // columns
    terms = like((pairs_here, vec_rows, transitions), F32)
    flops = 2 * vec_count * products * own_waves
    scratch = [pltpu.VMEM((columns, vec_rows, transitions), F32)]
    seconds = call(
        apply_second_kernel,
        [terms] + [like(terms.shape, BF16)] * (halves - 1),
        q_keep,
        q_far,
        *received,
        rho_second,
        flops=flops,
        scratch=scratch,
    )
    out_own, *out_msgs = call(
        apply_first_kernel,
        [like((2, *v.shape), v.dtype) for v in seconds],
        left_own,
        left_far,
        rho_first,
        *seconds,
        flops=flops,
        scratch=scratch,
    )
    received = [shift(out_msgs[s - 1], s) for s in range(1, halves)]
    placed = pl.pallas_call(
        functools.partial(send_kernel, groups=groups, halves=halves),
        in_specs=[smem] + [vmem] * halves,
        out_specs=vmem,
        out_shape=like(
            (groups * pairs_here, k_count // groups, vec_rows, transitions), BF16
        ),
        compiler_params=pltpu.CompilerParams(vmem_limit_bytes=4 * 2**20),
    )(pair_list.T, out_own, *received)
    return jnp.sum(exchange(placed).astype(F32), axis=0)


def solution(mesh):
    in_specs = (P(None, "pairs", "pw"), P(None, "pairs", None), P("pairs", "pw", None), P(), P())
    out_specs = P("pairs", "pw", None)
    return jax.shard_map(local, mesh=mesh, in_specs=in_specs, out_specs=out_specs, check_vma=False)
```

```python
import functools
import math

import jax
import jax.numpy as jnp
import numpy as np
from jax import lax
from jax.experimental import pallas as pl
from jax.experimental.pallas import tpu as pltpu
from jax.sharding import PartitionSpec as P

NV = 16
NC = 16
FINE = 64
BF16 = jnp.bfloat16
F32 = jnp.float32


def column_order(size):
    return np.concatenate([np.arange(0, size, 4), np.arange(2, size, 4), np.arange(1, size, 2)])


def phase_tables(points, waves, halves, columns):
    width, chunk = waves // columns, points // columns
    period, turn = 4 * points, math.pi / (2 * points)
    scale = math.sqrt(2.0 / points)
    seeds = []
    for j in range(halves):
        own = np.concatenate(
            [np.arange(c * width, (c + 1) * width) for c in range(j, columns, halves)]
        )
        own = own[column_order(own.size)].astype(np.int64)
        starts = np.concatenate(
            [
                np.arange((c * halves + (j ^ s)) * chunk, (c * halves + (j ^ s) + 1) * chunk, FINE)
                for s in range(halves // 2)
                for c in range(columns // halves)
            ]
        )
        coarse = (2 * starts[:, None] * own) % period * turn
        fine = ((2 * np.arange(FINE) + 1)[:, None] * own) % period * turn
        seeds.append(
            [
                np.concatenate([np.cos(coarse) * scale, np.cos(fine)]),
                np.concatenate([np.sin(coarse) * scale, np.sin(fine)]),
            ]
        )
    return np.array(seeds).astype(np.float32)


def one_hot_matrix(size, target):
    rows = lax.broadcasted_iota(jnp.int32, (size, size), 0)
    cols = lax.broadcasted_iota(jnp.int32, (size, size), 1)
    return jnp.where(target(rows) == cols, 1.0, 0.0).astype(BF16)


def interleave(size):
    part = size // 4
    return one_hot_matrix(
        size,
        lambda r: jnp.where(r < part, 4 * r, jnp.where(r < 2 * part, 4 * r - size + 2, 2 * r - size + 1)),
    )


def pieces(waves, i, size):
    part, quarter = size // 4, waves // 4
    yield i * part, part
    yield quarter + i * part, part
    yield 2 * quarter + 2 * i * part, 2 * part


def place(halves):
    w = lax.axis_index("pw")
    return lax.rem(w, halves), lax.div(w, halves)


def dot(a, b):
    return jnp.dot(a, b, preferred_element_type=F32)


def dot_nt(a, b):
    return lax.dot_general(a, b, (((1,), (1,)), ((), ())), preferred_element_type=F32)


def gather_kernel(
    requests, orbitals, far_vectors, out, held, vectors, load, store, fetch, *, halves
):
    count, slots, rows = out.shape[:3]
    chunk = orbitals.shape[2]
    fetched = pltpu.make_async_copy(far_vectors, vectors, fetch)
    fetched.start()

    def load_of(i, slot):
        return pltpu.make_async_copy(
            orbitals.at[requests[slot, i]], held.at[i, slot, :, pl.ds(0, chunk)], load.at[i, slot]
        )

    def start(i, carry):
        for slot in range(slots):
            load_of(i, slot).start()
        return carry

    lax.fori_loop(0, count, start, 0)
    x = place(halves)[1]
    fetched.wait()

    def pick(i, carry):
        for slot in range(slots):
            block = vectors[requests[slot, i]]
            held[i, slot, :, chunk:] = jnp.where(x == 0, block[:rows], block[rows:])
        return carry

    lax.fori_loop(0, count, pick, 0)

    def send(i, carry):
        for slot in range(slots):
            load_of(i, slot).wait()
        pltpu.make_async_copy(held.at[i], out.at[i], store.at[i]).start()
        return carry

    lax.fori_loop(0, count, send, 0)

    def end(i, carry):
        pltpu.make_async_copy(held.at[i], out.at[i], store.at[i]).wait()
        return carry

    lax.fori_loop(0, count, end, 0)


def table_kernel(seeds, table, *, block, chunk):
    half = table.shape[1]
    coarse = seeds.shape[1] - FINE
    per_chunk, rows = chunk // block, block // FINE
    for c in range(2):
        cols = slice(0, 2 * half) if c == 0 else slice(half, 2 * half)
        cb, sb = seeds[0, coarse:, cols], seeds[1, coarse:, cols]
        for t in range(table.shape[0] // (3 * block)):
            s, b = t // per_chunk, t % per_chunk

            def step(a, carry):
                row = (s * 2 + c) * per_chunk * rows + b * rows + a
                ca, sa = seeds[0, pl.ds(row, 1), :], seeds[1, pl.ds(row, 1), :]
                fresh = (ca[:, cols] * cb - sa[:, cols] * sb).astype(BF16)
                to = pl.multiple_of(3 * t * block + a * FINE, FINE)
                if c == 0:
                    table[pl.ds(to, FINE), :] = fresh[:, :half]
                    fresh = fresh[:, half:]
                to = pl.multiple_of((3 * t + 1 + c) * block + a * FINE, FINE)
                table[pl.ds(to, FINE), :] = fresh
                return carry

            lax.fori_loop(0, rows, step, 0, unroll=2)


def transform_kernel(*refs, halves, slot):
    parts, vec = refs[:halves], refs[halves]
    refs = refs[halves + 1 :]
    table_copies = []
    if slot == 0:
        far_table, rho_own, rho_msg, p_own, p_msg, table, sem = *refs[:6], refs[-1]
        for t in range(sem.shape[0]):
            span = pl.ds(t * (table.shape[0] // sem.shape[0]), table.shape[0] // sem.shape[0])
            table_copies.append(pltpu.make_async_copy(far_table.at[span], table.at[span], sem.at[t]))
            table_copies[-1].start()
    else:
        table, far_screened, rho, natural_out, screened = refs[:5]
        copy = pltpu.make_async_copy(far_screened, screened, refs[-1])
        copy.start()
    refs = refs[:-1]
    evens, odds, acc = refs[-3:]
    x = place(halves)[1]
    chunk = parts[0].shape[2]
    block = evens.shape[3]
    waves = acc.shape[1]
    half, quarter = waves // 2, waves // 4
    flip = one_hot_matrix(256, lambda r: 255 - r)
    per_chunk = chunk // block
    bands = parts[0].shape[1]
    count = halves // 2 * per_chunk

    def produce(t):
        s, b = t // per_chunk, t % per_chunk
        now = t % 2
        end = chunk - b * block
        near, back = [], []
        for c in range(2):
            mirror = parts[s ^ (halves - 1)]
            back.append(
                jnp.concatenate(
                    [
                        dot(mirror[1 - c, :, end - 256 * (i + 1) : end - 256 * i], flip)
                        for i in range(block // 256)
                    ],
                    axis=1,
                )
            )
            near.append(parts[s][c, :, b * block : (b + 1) * block].astype(F32))
        for v in range(NV):
            to = slice(v * NC, (v + 1) * NC)
            even = []
            for c in range(2):
                here = near[c][v : v + 1] * near[c][NV:bands]
                there = back[c][v : v + 1] * back[c][NV:bands]
                even.append(here + there)
                odds[now, to, c * block : (c + 1) * block] = (here - there).astype(BF16)
            evens[now, 0, to, :] = (even[0] + even[1]).astype(BF16)
            evens[now, 1, to, :] = (even[0] - even[1]).astype(BF16)

    def consume(t):
        now = t % 2
        for table_copy in table_copies[t : t + 1]:
            table_copy.wait()
        first, second, third = 3 * t * block, (3 * t + 1) * block, (3 * t + 3) * block
        terms = (
            dot(evens[now, 0], table[first:second, :quarter]),
            dot(evens[now, 1], table[first:second, quarter:]),
            dot(odds[now], table[second:third, :]),
        )
        for cols, term in zip((slice(0, quarter), slice(quarter, half), slice(half, waves)), terms):
            if t == 0:
                acc[:, cols] = term
            else:
                acc[:, cols] += term

    produce(0)
    for t in range(count):
        if t + 1 < count:
            produce(t + 1)
        consume(t)
    done = acc[...].astype(BF16)
    width = waves // 2
    proj = dot(vec[...], done).astype(BF16)
    order = interleave(width)

    def chunk_of(array, i):
        return jnp.concatenate([array[:, o : o + n] for o, n in pieces(waves, i, width)], axis=1)

    natural = [dot(chunk_of(proj, i), order).astype(BF16) for i in range(2)]
    if slot == 1:
        rho[...] = done
        natural_out[...] = jnp.concatenate(natural, axis=1)
        copy.wait()
    else:
        both = [chunk_of(done, i) for i in range(2)]
        rho_own[...] = jnp.where(x == 0, both[0], both[1])
        rho_msg[...] = jnp.where(x == 0, both[1], both[0])
        p_own[...] = jnp.where(x == 0, natural[0], natural[1])
        p_msg[...] = jnp.where(x == 0, natural[1], natural[0])


def back_kernel(p_own, p_far, screened, q_keep, q_part, *q_msgs):
    shifts = len(q_msgs) // 2 + 1
    j, x = place(shifts)
    width = p_own.shape[1]
    for rel in range(2):
        pair = x if rel == 0 else 1 - x
        first = (p_far if rel else p_own)[...]
        for s in range(shifts):
            for c in range(2):
                start = pl.multiple_of((c * shifts + (j ^ s)) * width, width)
                term = dot(first, screened[pair, :, pl.ds(start, width)])
                cols = slice(c * width, (c + 1) * width)
                if s == 0:
                    (q_part if rel else q_keep)[:, cols] = term
                else:
                    q_msgs[2 * (s - 1) + rel][:, cols] = term.astype(BF16)


def cut(value, scratch, outs):
    shifts = len(outs)
    j = place(shifts)[0]
    scratch[...] = value.reshape(scratch.shape)
    for s in range(shifts):
        for c in range(2):
            outs[s][c] = scratch[c * shifts + (j ^ s)].astype(outs[s].dtype)


def forward_kernel(*refs, shifts):
    sources, refs = refs[: 2 * shifts], refs[2 * shifts :]
    rho_own, rho_far, screened = refs[:3]
    outs, scratch = refs[3:-1], refs[-1]
    j, x = place(shifts)
    width = rho_own.shape[1]
    order = interleave(width)
    for rel in range(2):
        pair = x if rel == 0 else 1 - x
        total = None
        for s in range(shifts):
            source = sources[rel * shifts + s]
            for c in range(2):
                start = pl.multiple_of((c * shifts + (j ^ s)) * width, width)
                term = dot_nt(
                    source[:, c * width : (c + 1) * width], screened[pair, :, pl.ds(start, width)]
                )
                total = term if total is None else total + term
        weight = dot_nt(total.astype(BF16), order).astype(BF16)
        products = (rho_far if rel else rho_own)[...]
        cut(dot_nt(weight, products), scratch.at[rel], [out.at[rel] for out in outs])


def second_kernel(q_keep, q_far, *refs, shifts):
    received, rho = refs[: shifts - 1], refs[shifts - 1]
    others, outs, scratch = refs[shifts : 2 * shifts], refs[2 * shifts : -1], refs[-1]
    weight = q_keep[...] + q_far[...].astype(F32)
    for part in received:
        weight = weight + part[...].astype(F32)
    weight = weight.astype(BF16)
    waves = rho.shape[1]
    width = waves // 2
    order = interleave(width)
    parts = [
        dot_nt(weight[:, width * i : width * (i + 1)], order).astype(BF16) for i in range(2)
    ]
    cuts = (0, width // 4, width // 2, width)
    sorted_weight = jnp.concatenate(
        [p[:, lo:hi] for lo, hi in zip(cuts, cuts[1:]) for p in parts], axis=1
    )
    cut(dot_nt(sorted_weight, rho[...]), scratch, [out.at[2] for out in outs])
    for out, other in zip(outs, others):
        out[:2] = other[...]


def send_kernel(pairs, own, *refs, groups, halves):
    received, out = refs[:-1], refs[-1]
    parts = own.shape[1]
    x = place(halves)[1]
    first = lax.axis_index("pairs") * parts
    spots = ((0, first + x), (0, first + 1 - x), (1, first + x))
    owned = out.shape[1]
    total = own[...]
    for part in received:
        total = total + part[...].astype(F32)
    for k in range(groups * owned):
        for part in range(parts):
            value = jnp.zeros(own.shape[2:], F32)
            for term, (slot, index) in enumerate(spots):
                value = value + jnp.where(pairs[slot, index] == k, total[term, part], 0.0)
            out[k // owned * parts + part, k % owned] = value.astype(BF16)


def local(orbitals, vectors, screened, pair_list, band_order):
    groups = lax.axis_size("pairs")
    columns = lax.axis_size("pw")
    pairs_here = screened.shape[0]
    halves = columns // pairs_here
    both = ("pairs", "pw")
    w = lax.axis_index("pw")
    k_count, band_here, chunk = orbitals.shape
    points = chunk * columns
    waves = screened.shape[2]
    width = waves // columns
    own_waves = width * pairs_here
    transitions = vectors.shape[2]
    vec_count = vectors.shape[1] * groups
    vec_part = vectors.shape[1] // pairs_here
    bands = band_here * groups
    members = [
        [gg * columns + xx * halves + jj for gg in range(groups) for xx in range(pairs_here)]
        for jj in range(halves)
    ]

    def exchange(value):
        return lax.all_to_all(value, both, 0, 0, tiled=True, axis_index_groups=members)

    def shift(value, s):
        return lax.ppermute(value, "pw", [(i, i ^ s) for i in range(columns)])

    def call(kernel, outs, *args, flops=0, scratch=(), limit=4, far=0, cost=None):
        moved = cost or sum(math.prod(v.shape) * v.dtype.itemsize for v in (*args, *outs))
        return pl.pallas_call(
            kernel,
            in_specs=[vmem] * (len(args) - far) + [hbm] * far,
            out_specs=[vmem] * len(outs),
            out_shape=list(outs),
            scratch_shapes=list(scratch),
            compiler_params=pltpu.CompilerParams(vmem_limit_bytes=limit * 2**20),
            cost_estimate=pl.CostEstimate(flops=flops, bytes_accessed=moved, transcendentals=0),
        )(*args)

    smem = pl.BlockSpec(memory_space=pltpu.SMEM)
    vmem = pl.BlockSpec(memory_space=pltpu.VMEM)
    hbm = pl.BlockSpec(memory_space=pltpu.HBM)
    like = jax.ShapeDtypeStruct

    slots = 2 * groups * pairs_here
    sent = pl.pallas_call(
        functools.partial(gather_kernel, halves=halves),
        in_specs=[smem, hbm, hbm],
        out_specs=hbm,
        out_shape=like((slots // 2, 2, band_here, chunk + transitions), BF16),
        scratch_shapes=[
            pltpu.VMEM((slots // 2, 2, band_here, chunk + transitions), BF16),
            pltpu.VMEM(vectors.shape, BF16),
            pltpu.SemaphoreType.DMA((slots // 2, 2)),
            pltpu.SemaphoreType.DMA((slots // 2,)),
            pltpu.SemaphoreType.DMA,
        ],
        compiler_params=pltpu.CompilerParams(vmem_limit_bytes=60 * 2**20),
    )(pair_list.T, orbitals, vectors)
    got = exchange(sent).reshape(groups, pairs_here, 2, band_here, chunk + transitions)
    seeds = lax.dynamic_index_in_dim(
        jnp.asarray(phase_tables(points, waves, halves, columns)), w % halves, keepdims=False
    )
    vec = got[..., chunk:].transpose(2, 0, 1, 3, 4).reshape(2, vec_count, transitions)
    picker = (band_order[:, None] == jnp.arange(bands, dtype=jnp.int32)[None, :]).astype(BF16)
    half_waves = own_waves // 2
    block = min(1024, chunk)
    (table,) = call(
        functools.partial(table_kernel, block=block, chunk=chunk),
        [like((3 * points // 4, half_waves), BF16)],
        seeds,
        flops=3 * points * half_waves,
    )
    picker, table = lax.optimization_barrier((picker, table))
    psi = jnp.einsum(
        "gbn,gxlbr->lxnr",
        picker.reshape(groups, band_here, bands),
        got[..., :chunk],
        preferred_element_type=F32,
    ).astype(BF16)
    products = NV * NC

    def transform(slot, outs, *args):
        parts = [psi[slot]] + [shift(psi[slot], s) for s in range(1, halves)]
        return call(
            functools.partial(transform_kernel, halves=halves, slot=slot),
            outs,
            *parts,
            vec[slot],
            *args,
            flops=products * points * own_waves,
            scratch=[
                pltpu.VMEM((2, 2, products, block), BF16),
                pltpu.VMEM((2, products, 2 * block), BF16),
                pltpu.VMEM((products, own_waves), F32),
            ]
            + [pltpu.SemaphoreType.DMA if slot else pltpu.SemaphoreType.DMA((points // 4 // block,))],
            limit=24 if slot else 36,
            far=1,
        )

    part = like((products, width), BF16)
    p_part = like((vec_count, width), BF16)
    rho_own, rho_msg, p_own, p_msg, table = transform(
        0, [part, part, p_part, p_part, like(table.shape, BF16)], table
    )
    p_far = shift(p_msg, halves)
    rho_far = shift(rho_msg, halves)
    full = like((vec_count, own_waves), BF16)
    rho, p_second, screened = transform(
        1,
        [like((products, own_waves), BF16), full, like(screened.shape, BF16)],
        table,
        screened,
    )

    p_own, p_second = lax.optimization_barrier((p_own, p_second))
    far = shift(p_second, halves)
    near = [shift(p_second, s) for s in range(1, halves)]
    fars = [shift(far, s) for s in range(1, halves)]
    flops = 4 * vec_count * width * waves
    partial_q = like((vec_count, own_waves), F32)
    q_keep, q_part, *q_msgs = call(
        back_kernel,
        [partial_q] * 2 + [like((vec_count, own_waves), BF16)] * (2 * (halves - 1)),
        p_own,
        p_far,
        screened,
        cost=1,
    )
    q_msgs, rho_far = lax.optimization_barrier((q_msgs, rho_far))
    received = [
        [shift(q_msgs[2 * (s - 1) + rel], s) for s in range(1, halves)] for rel in range(2)
    ]
    q_send = (q_part + sum(v.astype(F32) for v in received[1])).astype(BF16)
    q_far = shift(q_send, halves)
    vec_rows = vec_count // columns
    shape = (pairs_here, vec_rows, transitions)
    forward = call(
        functools.partial(forward_kernel, shifts=halves),
        [like((2, *shape), F32)] + [like((2, *shape), BF16)] * (halves - 1),
        p_second,
        *near,
        far,
        *fars,
        rho_own,
        rho_far,
        screened,
        cost=1,
        scratch=[pltpu.VMEM((2, columns, vec_rows, transitions), F32)],
    )
    out_own, *out_msgs = call(
        functools.partial(second_kernel, shifts=halves),
        [like((3, *shape), F32)] + [like((3, *shape), BF16)] * (halves - 1),
        q_keep,
        q_far,
        *received[0],
        rho,
        *forward,
        flops=2 * vec_count * products * own_waves,
        scratch=[pltpu.VMEM((columns, vec_rows, transitions), F32)],
    )

    received = [shift(out_msgs[s - 1], s) for s in range(1, halves)]
    placed = pl.pallas_call(
        functools.partial(send_kernel, groups=groups, halves=halves),
        in_specs=[smem] + [vmem] * halves,
        out_specs=vmem,
        out_shape=like(
            (groups * pairs_here, k_count // groups, vec_rows, transitions), BF16
        ),
        compiler_params=pltpu.CompilerParams(vmem_limit_bytes=4 * 2**20),
    )(pair_list.T, out_own, *received)
    return jnp.sum(exchange(placed).astype(F32), axis=0)


def solution(mesh):
    in_specs = (P(None, "pairs", "pw"), P(None, "pairs", None), P("pairs", "pw", None), P(), P())
    out_specs = P("pairs", "pw", None)
    return jax.shard_map(local, mesh=mesh, in_specs=in_specs, out_specs=out_specs, check_vma=False)
```

```python
import functools
import math

import jax
import jax.numpy as jnp
import numpy as np
from jax import lax
from jax.experimental import pallas as pl
from jax.experimental.pallas import tpu as pltpu
from jax.sharding import PartitionSpec as P

NV = 16
NC = 16
FINE = 64
BF16 = jnp.bfloat16
F32 = jnp.float32


def column_order(size):
    return np.concatenate([np.arange(0, size, 4), np.arange(2, size, 4), np.arange(1, size, 2)])


def phase_tables(points, waves, halves, columns):
    width, chunk = waves // columns, points // columns
    period, turn = 4 * points, math.pi / (2 * points)
    scale = math.sqrt(2.0 / points)
    seeds = []
    for j in range(halves):
        own = np.concatenate(
            [np.arange(c * width, (c + 1) * width) for c in range(j, columns, halves)]
        )
        own = own[column_order(own.size)].astype(np.int64)
        starts = np.concatenate(
            [
                np.arange((c * halves + (j ^ s)) * chunk, (c * halves + (j ^ s) + 1) * chunk, FINE)
                for s in range(halves // 2)
                for c in range(columns // halves)
            ]
        )
        coarse = (2 * starts[:, None] * own) % period * turn
        fine = ((2 * np.arange(FINE) + 1)[:, None] * own) % period * turn
        seeds.append(
            [
                np.concatenate([np.cos(coarse) * scale, np.cos(fine)]),
                np.concatenate([np.sin(coarse) * scale, np.sin(fine)]),
            ]
        )
    return np.array(seeds).astype(np.float32)


def one_hot_matrix(size, target):
    rows = lax.broadcasted_iota(jnp.int32, (size, size), 0)
    cols = lax.broadcasted_iota(jnp.int32, (size, size), 1)
    return jnp.where(target(rows) == cols, 1.0, 0.0).astype(BF16)


def interleave(size):
    part = size // 4
    return one_hot_matrix(
        size,
        lambda r: jnp.where(r < part, 4 * r, jnp.where(r < 2 * part, 4 * r - size + 2, 2 * r - size + 1)),
    )


def pieces(waves, i, size):
    part, quarter = size // 4, waves // 4
    yield i * part, part
    yield quarter + i * part, part
    yield 2 * quarter + 2 * i * part, 2 * part


def place(halves):
    w = lax.axis_index("pw")
    return lax.rem(w, halves), lax.div(w, halves)


def dot(a, b):
    return jnp.dot(a, b, preferred_element_type=F32)


def dot_nt(a, b):
    return lax.dot_general(a, b, (((1,), (1,)), ((), ())), preferred_element_type=F32)


def gather_kernel(
    requests, orbitals, far_vectors, out, held, vectors, load, store, fetch, *, halves
):
    count, slots, rows = out.shape[:3]
    chunk = orbitals.shape[2]
    fetched = pltpu.make_async_copy(far_vectors, vectors, fetch)
    fetched.start()

    def load_of(i, slot):
        return pltpu.make_async_copy(
            orbitals.at[requests[slot, i]], held.at[i, slot, :, pl.ds(0, chunk)], load.at[i, slot]
        )

    def start(i, carry):
        for slot in range(slots):
            load_of(i, slot).start()
        return carry

    lax.fori_loop(0, count, start, 0)
    x = place(halves)[1]
    fetched.wait()

    def pick(i, carry):
        for slot in range(slots):
            block = vectors[requests[slot, i]]
            held[i, slot, :, chunk:] = jnp.where(x == 0, block[:rows], block[rows:])
        return carry

    lax.fori_loop(0, count, pick, 0)

    def send(i, carry):
        for slot in range(slots):
            load_of(i, slot).wait()
        pltpu.make_async_copy(held.at[i], out.at[i], store.at[i]).start()
        return carry

    lax.fori_loop(0, count, send, 0)

    def end(i, carry):
        pltpu.make_async_copy(held.at[i], out.at[i], store.at[i]).wait()
        return carry

    lax.fori_loop(0, count, end, 0)


def table_kernel(seeds, table, *, block, chunk):
    half = table.shape[1]
    coarse = seeds.shape[1] - FINE
    per_chunk, rows = chunk // block, block // FINE
    for c in range(2):
        cols = slice(0, 2 * half) if c == 0 else slice(half, 2 * half)
        cb, sb = seeds[0, coarse:, cols], seeds[1, coarse:, cols]
        for t in range(table.shape[0] // (3 * block)):
            s, b = t // per_chunk, t % per_chunk

            def step(a, carry):
                row = (s * 2 + c) * per_chunk * rows + b * rows + a
                ca, sa = seeds[0, pl.ds(row, 1), :], seeds[1, pl.ds(row, 1), :]
                fresh = (ca[:, cols] * cb - sa[:, cols] * sb).astype(BF16)
                to = pl.multiple_of(3 * t * block + a * FINE, FINE)
                if c == 0:
                    table[pl.ds(to, FINE), :] = fresh[:, :half]
                    fresh = fresh[:, half:]
                to = pl.multiple_of((3 * t + 1 + c) * block + a * FINE, FINE)
                table[pl.ds(to, FINE), :] = fresh
                return carry

            lax.fori_loop(0, rows, step, 0, unroll=2)


def transform_kernel(*refs, halves, slot):
    parts, refs = refs[:halves], refs[halves:]
    table_copies = []
    if slot == 0:
        vec, far_table, rho_own, rho_msg, table, sem = *refs[:5], refs[-1]
        for t in range(sem.shape[0]):
            span = pl.ds(t * (table.shape[0] // sem.shape[0]), table.shape[0] // sem.shape[0])
            table_copies.append(pltpu.make_async_copy(far_table.at[span], table.at[span], sem.at[t]))
            table_copies[-1].start()
    else:
        vec, table, far_screened, rho, natural_out, screened = refs[:6]
        copy = pltpu.make_async_copy(far_screened, screened, refs[-1])
        copy.start()
    refs = refs[:-1]
    evens, odds, acc = refs[-3:]
    x = place(halves)[1]
    chunk = parts[0].shape[2]
    block = evens.shape[3]
    waves = acc.shape[1]
    half, quarter = waves // 2, waves // 4
    flip = one_hot_matrix(256, lambda r: 255 - r)
    per_chunk = chunk // block
    bands = parts[0].shape[1]
    count = halves // 2 * per_chunk

    def produce(t):
        s, b = t // per_chunk, t % per_chunk
        now = t % 2
        end = chunk - b * block
        near, back = [], []
        for c in range(2):
            mirror = parts[s ^ (halves - 1)]
            back.append(
                jnp.concatenate(
                    [
                        dot(mirror[1 - c, :, end - 256 * (i + 1) : end - 256 * i], flip)
                        for i in range(block // 256)
                    ],
                    axis=1,
                )
            )
            near.append(parts[s][c, :, b * block : (b + 1) * block].astype(F32))
        for v in range(NV):
            to = slice(v * NC, (v + 1) * NC)
            even = []
            for c in range(2):
                here = near[c][v : v + 1] * near[c][NV:bands]
                there = back[c][v : v + 1] * back[c][NV:bands]
                even.append(here + there)
                odds[now, to, c * block : (c + 1) * block] = (here - there).astype(BF16)
            evens[now, 0, to, :] = (even[0] + even[1]).astype(BF16)
            evens[now, 1, to, :] = (even[0] - even[1]).astype(BF16)

    def consume(t):
        now = t % 2
        for table_copy in table_copies[t : t + 1]:
            table_copy.wait()
        first, second, third = 3 * t * block, (3 * t + 1) * block, (3 * t + 3) * block
        terms = (
            dot(evens[now, 0], table[first:second, :quarter]),
            dot(evens[now, 1], table[first:second, quarter:]),
            dot(odds[now], table[second:third, :]),
        )
        for cols, term in zip((slice(0, quarter), slice(quarter, half), slice(half, waves)), terms):
            if t == 0:
                acc[:, cols] = term
            else:
                acc[:, cols] += term

    produce(0)
    for t in range(count):
        if t + 1 < count:
            produce(t + 1)
        consume(t)
    done = acc[...].astype(BF16)
    both = [
        jnp.concatenate([done[:, o : o + n] for o, n in pieces(waves, i, waves // 2)], axis=1)
        for i in range(2)
    ]
    if slot == 1:
        rho[...] = done
        order = interleave(waves // 2)
        natural_out[...] = jnp.concatenate([project(vec, part, order) for part in both], axis=1)
        copy.wait()
    else:
        rho_own[...] = jnp.where(x == 0, both[0], both[1])
        rho_msg[: NV * NC] = jnp.where(x == 0, both[1], both[0])
        rho_msg[NV * NC :] = pack(vec[...], rho_msg.shape[1])


def pack(array, width):
    rows, cols = array.shape
    if cols < width:
        step = rows * cols // width
        return jnp.concatenate([array[i : i + step] for i in range(0, rows, step)], axis=1)
    return jnp.concatenate([array[:, i : i + width] for i in range(0, cols, width)], axis=0)


def project(vec, rho, order):
    return dot(dot(vec[...], rho).astype(BF16), order).astype(BF16)


def back_kernel(vec_own, rho_own, rho_far, screened, q_keep, q_part, *q_msgs):
    shifts = len(q_msgs) // 2 + 1
    j, x = place(shifts)
    width = rho_own.shape[1]
    order = interleave(width)
    for rel in range(2):
        pair = x if rel == 0 else 1 - x
        if rel:
            vec = pack(rho_far[NV * NC :, :], vec_own.shape[1])
            first = project(vec, rho_far[: NV * NC, :], order)
        else:
            first = project(vec_own, rho_own[...], order)
        for s in range(shifts):
            for c in range(2):
                start = pl.multiple_of((c * shifts + (j ^ s)) * width, width)
                term = dot(first, screened[pair, :, pl.ds(start, width)])
                cols = slice(c * width, (c + 1) * width)
                if s == 0:
                    (q_part if rel else q_keep)[:, cols] = term
                else:
                    q_msgs[2 * (s - 1) + rel][:, cols] = term.astype(BF16)


def cut(value, scratch, outs):
    shifts = len(outs)
    j = place(shifts)[0]
    scratch[...] = value.reshape(scratch.shape)
    for s in range(shifts):
        for c in range(2):
            outs[s][c] = scratch[c * shifts + (j ^ s)].astype(outs[s].dtype)


def forward_kernel(*refs, shifts):
    sources, refs = refs[: 2 * shifts], refs[2 * shifts :]
    rho_own, rho_far, screened = refs[:3]
    outs, scratch = refs[3:-1], refs[-1]
    j, x = place(shifts)
    width = rho_own.shape[1]
    order = interleave(width)
    for rel in range(2):
        pair = x if rel == 0 else 1 - x
        total = None
        for s in range(shifts):
            source = sources[rel * shifts + s]
            for c in range(2):
                start = pl.multiple_of((c * shifts + (j ^ s)) * width, width)
                term = dot_nt(
                    source[:, c * width : (c + 1) * width], screened[pair, :, pl.ds(start, width)]
                )
                total = term if total is None else total + term
        weight = dot_nt(total.astype(BF16), order).astype(BF16)
        products = (rho_far if rel else rho_own)[: NV * NC, :]
        cut(dot_nt(weight, products), scratch.at[rel], [out.at[rel] for out in outs])


def second_kernel(q_keep, q_far, *refs, shifts):
    received, rho = refs[: shifts - 1], refs[shifts - 1]
    others, outs, scratch = refs[shifts : 2 * shifts], refs[2 * shifts : -1], refs[-1]
    weight = q_keep[...] + q_far[...].astype(F32)
    for part in received:
        weight = weight + part[...].astype(F32)
    weight = weight.astype(BF16)
    waves = rho.shape[1]
    width = waves // 2
    order = interleave(width)
    parts = [
        dot_nt(weight[:, width * i : width * (i + 1)], order).astype(BF16) for i in range(2)
    ]
    cuts = (0, width // 4, width // 2, width)
    sorted_weight = jnp.concatenate(
        [p[:, lo:hi] for lo, hi in zip(cuts, cuts[1:]) for p in parts], axis=1
    )
    cut(dot_nt(sorted_weight, rho[...]), scratch, [out.at[2] for out in outs])
    for out, other in zip(outs, others):
        out[:2] = other[...]


def send_kernel(pairs, own, *refs, groups, halves):
    received, out = refs[:-1], refs[-1]
    parts = own.shape[1]
    x = place(halves)[1]
    first = lax.axis_index("pairs") * parts
    spots = ((0, first + x), (0, first + 1 - x), (1, first + x))
    owned = out.shape[1]
    total = own[...]
    for part in received:
        total = total + part[...].astype(F32)
    for k in range(groups * owned):
        for part in range(parts):
            value = jnp.zeros(own.shape[2:], F32)
            for term, (slot, index) in enumerate(spots):
                value = value + jnp.where(pairs[slot, index] == k, total[term, part], 0.0)
            out[k // owned * parts + part, k % owned] = value.astype(BF16)


def local(orbitals, vectors, screened, pair_list, band_order):
    groups = lax.axis_size("pairs")
    columns = lax.axis_size("pw")
    pairs_here = screened.shape[0]
    halves = columns // pairs_here
    both = ("pairs", "pw")
    w = lax.axis_index("pw")
    k_count, band_here, chunk = orbitals.shape
    points = chunk * columns
    waves = screened.shape[2]
    width = waves // columns
    own_waves = width * pairs_here
    transitions = vectors.shape[2]
    vec_count = vectors.shape[1] * groups
    vec_part = vectors.shape[1] // pairs_here
    bands = band_here * groups
    members = [
        [gg * columns + xx * halves + jj for gg in range(groups) for xx in range(pairs_here)]
        for jj in range(halves)
    ]

    def exchange(value):
        return lax.all_to_all(value, both, 0, 0, tiled=True, axis_index_groups=members)

    def shift(value, s):
        return lax.ppermute(value, "pw", [(i, i ^ s) for i in range(columns)])

    def call(kernel, outs, *args, flops=0, scratch=(), limit=4, far=0, cost=None):
        moved = cost or sum(math.prod(v.shape) * v.dtype.itemsize for v in (*args, *outs))
        return pl.pallas_call(
            kernel,
            in_specs=[vmem] * (len(args) - far) + [hbm] * far,
            out_specs=[vmem] * len(outs),
            out_shape=list(outs),
            scratch_shapes=list(scratch),
            compiler_params=pltpu.CompilerParams(vmem_limit_bytes=limit * 2**20),
            cost_estimate=pl.CostEstimate(flops=flops, bytes_accessed=moved, transcendentals=0),
        )(*args)

    smem = pl.BlockSpec(memory_space=pltpu.SMEM)
    vmem = pl.BlockSpec(memory_space=pltpu.VMEM)
    hbm = pl.BlockSpec(memory_space=pltpu.HBM)
    like = jax.ShapeDtypeStruct

    slots = 2 * groups * pairs_here
    sent = pl.pallas_call(
        functools.partial(gather_kernel, halves=halves),
        in_specs=[smem, hbm, hbm],
        out_specs=hbm,
        out_shape=like((slots // 2, 2, band_here, chunk + transitions), BF16),
        scratch_shapes=[
            pltpu.VMEM((slots // 2, 2, band_here, chunk + transitions), BF16),
            pltpu.VMEM(vectors.shape, BF16),
            pltpu.SemaphoreType.DMA((slots // 2, 2)),
            pltpu.SemaphoreType.DMA((slots // 2,)),
            pltpu.SemaphoreType.DMA,
        ],
        compiler_params=pltpu.CompilerParams(vmem_limit_bytes=60 * 2**20),
    )(pair_list.T, orbitals, vectors)
    got = exchange(sent).reshape(groups, pairs_here, 2, band_here, chunk + transitions)
    seeds = lax.dynamic_index_in_dim(
        jnp.asarray(phase_tables(points, waves, halves, columns)), w % halves, keepdims=False
    )
    vec = got[..., chunk:].transpose(2, 0, 1, 3, 4).reshape(2, vec_count, transitions)
    picker = (band_order[:, None] == jnp.arange(bands, dtype=jnp.int32)[None, :]).astype(BF16)
    half_waves = own_waves // 2
    block = min(1024, chunk)
    (table,) = call(
        functools.partial(table_kernel, block=block, chunk=chunk),
        [like((3 * points // 4, half_waves), BF16)],
        seeds,
        flops=3 * points * half_waves,
    )
    picker, table = lax.optimization_barrier((picker, table))
    psi = jnp.einsum(
        "gbn,gxlbr->lxnr",
        picker.reshape(groups, band_here, bands),
        got[..., :chunk],
        preferred_element_type=F32,
    ).astype(BF16)
    products = NV * NC

    def transform(slot, outs, *args):
        parts = [psi[slot]] + [shift(psi[slot], s) for s in range(1, halves)]
        return call(
            functools.partial(transform_kernel, halves=halves, slot=slot),
            outs,
            *parts,
            *args,
            flops=products * points * own_waves,
            scratch=[
                pltpu.VMEM((2, 2, products, block), BF16),
                pltpu.VMEM((2, products, 2 * block), BF16),
                pltpu.VMEM((products, own_waves), F32),
            ]
            + [pltpu.SemaphoreType.DMA if slot else pltpu.SemaphoreType.DMA((points // 4 // block,))],
            limit=24 if slot else 36,
            far=1,
        )

    part = like((products, width), BF16)
    packed = like((products + vec_count * transitions // width, width), BF16)
    rho_own, rho_msg, table = transform(0, [part, packed, like(table.shape, BF16)], vec[0], table)
    rho_far = shift(rho_msg, halves)
    full = like((vec_count, own_waves), BF16)
    rho, p_second, screened = transform(
        1,
        [like((products, own_waves), BF16), full, like(screened.shape, BF16)],
        vec[1],
        table,
        screened,
    )

    rho_own, p_second = lax.optimization_barrier((rho_own, p_second))
    far = shift(p_second, halves)
    near = [shift(p_second, s) for s in range(1, halves)]
    fars = [shift(far, s) for s in range(1, halves)]
    flops = 4 * vec_count * width * waves
    partial_q = like((vec_count, own_waves), F32)
    q_keep, q_part, *q_msgs = call(
        back_kernel,
        [partial_q] * 2 + [like((vec_count, own_waves), BF16)] * (2 * (halves - 1)),
        vec[0],
        rho_own,
        rho_far,
        screened,
        cost=1,
    )
    received = [
        [shift(q_msgs[2 * (s - 1) + rel], s) for s in range(1, halves)] for rel in range(2)
    ]
    q_send = (q_part + sum(v.astype(F32) for v in received[1])).astype(BF16)
    q_far = shift(q_send, halves)
    vec_rows = vec_count // columns
    shape = (pairs_here, vec_rows, transitions)
    forward = call(
        functools.partial(forward_kernel, shifts=halves),
        [like((2, *shape), F32)] + [like((2, *shape), BF16)] * (halves - 1),
        p_second,
        *near,
        far,
        *fars,
        rho_own,
        rho_far,
        screened,
        cost=1,
        scratch=[pltpu.VMEM((2, columns, vec_rows, transitions), F32)],
    )
    out_own, *out_msgs = call(
        functools.partial(second_kernel, shifts=halves),
        [like((3, *shape), F32)] + [like((3, *shape), BF16)] * (halves - 1),
        q_keep,
        q_far,
        *received[0],
        rho,
        *forward,
        flops=2 * vec_count * products * own_waves,
        scratch=[pltpu.VMEM((columns, vec_rows, transitions), F32)],
    )

    received = [shift(out_msgs[s - 1], s) for s in range(1, halves)]
    placed = pl.pallas_call(
        functools.partial(send_kernel, groups=groups, halves=halves),
        in_specs=[smem] + [vmem] * halves,
        out_specs=vmem,
        out_shape=like(
            (groups * pairs_here, k_count // groups, vec_rows, transitions), BF16
        ),
        compiler_params=pltpu.CompilerParams(vmem_limit_bytes=4 * 2**20),
    )(pair_list.T, out_own, *received)
    return jnp.sum(exchange(placed).astype(F32), axis=0)


def solution(mesh):
    in_specs = (P(None, "pairs", "pw"), P(None, "pairs", None), P("pairs", "pw", None), P(), P())
    out_specs = P("pairs", "pw", None)
    return jax.shard_map(local, mesh=mesh, in_specs=in_specs, out_specs=out_specs, check_vma=False)
```

```python
import functools
import math

import jax
import jax.numpy as jnp
import numpy as np
from jax import lax
from jax.experimental import pallas as pl
from jax.experimental.pallas import tpu as pltpu
from jax.sharding import PartitionSpec as P

NV = 16
NC = 16
FINE = 64
BF16 = jnp.bfloat16
F32 = jnp.float32


def column_order(size):
    return np.concatenate([np.arange(0, size, 4), np.arange(2, size, 4), np.arange(1, size, 2)])


def phase_tables(points, waves, halves, columns):
    width, chunk = waves // columns, points // columns
    period, turn = 4 * points, math.pi / (2 * points)
    scale = math.sqrt(2.0 / points)
    seeds = []
    for j in range(halves):
        own = np.concatenate(
            [np.arange(c * width, (c + 1) * width) for c in range(j, columns, halves)]
        )
        own = own[column_order(own.size)].astype(np.int64)
        starts = np.concatenate(
            [
                np.arange((c * halves + (j ^ s)) * chunk, (c * halves + (j ^ s) + 1) * chunk, FINE)
                for s in range(halves // 2)
                for c in range(columns // halves)
            ]
        )
        coarse = (2 * starts[:, None] * own) % period * turn
        fine = ((2 * np.arange(FINE) + 1)[:, None] * own) % period * turn
        seeds.append(
            [
                np.concatenate([np.cos(coarse) * scale, np.cos(fine)]),
                np.concatenate([np.sin(coarse) * scale, np.sin(fine)]),
            ]
        )
    return np.array(seeds).astype(np.float32)


def one_hot_matrix(size, target):
    rows = lax.broadcasted_iota(jnp.int32, (size, size), 0)
    cols = lax.broadcasted_iota(jnp.int32, (size, size), 1)
    return jnp.where(target(rows) == cols, 1.0, 0.0).astype(BF16)


def interleave(size):
    part = size // 4
    return one_hot_matrix(
        size,
        lambda r: jnp.where(r < part, 4 * r, jnp.where(r < 2 * part, 4 * r - size + 2, 2 * r - size + 1)),
    )


def pieces(waves, i, size):
    part, quarter = size // 4, waves // 4
    yield i * part, part
    yield quarter + i * part, part
    yield 2 * quarter + 2 * i * part, 2 * part


def place(halves):
    w = lax.axis_index("pw")
    return lax.rem(w, halves), lax.div(w, halves)


def dot(a, b):
    return jnp.dot(a, b, preferred_element_type=F32)


def dot_nt(a, b):
    return lax.dot_general(a, b, (((1,), (1,)), ((), ())), preferred_element_type=F32)


def gather_kernel(
    requests, orbitals, far_vectors, out, held, vectors, load, store, fetch, *, halves
):
    count, slots, rows = out.shape[:3]
    chunk = orbitals.shape[2]
    fetched = pltpu.make_async_copy(far_vectors, vectors, fetch)
    fetched.start()

    def load_of(i, slot):
        return pltpu.make_async_copy(
            orbitals.at[requests[slot, i]], held.at[i, slot, :, pl.ds(0, chunk)], load.at[i, slot]
        )

    def start(i, carry):
        for slot in range(slots):
            load_of(i, slot).start()
        return carry

    lax.fori_loop(0, count, start, 0)
    x = place(halves)[1]
    fetched.wait()

    def pick(i, carry):
        for slot in range(slots):
            block = vectors[requests[slot, i]]
            held[i, slot, :, chunk:] = jnp.where(x == 0, block[:rows], block[rows:])
        return carry

    lax.fori_loop(0, count, pick, 0)

    def send(i, carry):
        for slot in range(slots):
            load_of(i, slot).wait()
        pltpu.make_async_copy(held.at[i], out.at[i], store.at[i]).start()
        return carry

    lax.fori_loop(0, count, send, 0)

    def end(i, carry):
        pltpu.make_async_copy(held.at[i], out.at[i], store.at[i]).wait()
        return carry

    lax.fori_loop(0, count, end, 0)


def table_kernel(seeds, table, *, block, chunk):
    half = table.shape[1]
    coarse = seeds.shape[1] - FINE
    per_chunk, rows = chunk // block, block // FINE
    for c in range(2):
        cols = slice(0, 2 * half) if c == 0 else slice(half, 2 * half)
        cb, sb = seeds[0, coarse:, cols], seeds[1, coarse:, cols]
        for t in range(table.shape[0] // (3 * block)):
            s, b = t // per_chunk, t % per_chunk

            def step(a, carry):
                row = (s * 2 + c) * per_chunk * rows + b * rows + a
                ca, sa = seeds[0, pl.ds(row, 1), :], seeds[1, pl.ds(row, 1), :]
                fresh = (ca[:, cols] * cb - sa[:, cols] * sb).astype(BF16)
                to = pl.multiple_of(3 * t * block + a * FINE, FINE)
                if c == 0:
                    table[pl.ds(to, FINE), :] = fresh[:, :half]
                    fresh = fresh[:, half:]
                to = pl.multiple_of((3 * t + 1 + c) * block + a * FINE, FINE)
                table[pl.ds(to, FINE), :] = fresh
                return carry

            lax.fori_loop(0, rows, step, 0, unroll=2)


def transform_kernel(*refs, halves, slot):
    parts, refs = refs[:halves], refs[halves:]
    table_copies = []
    if slot == 0:
        vec, far_table, rho_own, rho_msg, table, sem = *refs[:5], refs[-1]
        for t in range(sem.shape[0]):
            span = pl.ds(t * (table.shape[0] // sem.shape[0]), table.shape[0] // sem.shape[0])
            table_copies.append(pltpu.make_async_copy(far_table.at[span], table.at[span], sem.at[t]))
            table_copies[-1].start()
    else:
        vec, table, far_screened, rho, natural_out, screened = refs[:6]
        copy = pltpu.make_async_copy(far_screened, screened, refs[-1])
        copy.start()
    refs = refs[:-1]
    evens, odds, acc = refs[-3:]
    x = place(halves)[1]
    chunk = parts[0].shape[2]
    block = evens.shape[3]
    waves = acc.shape[1]
    half, quarter = waves // 2, waves // 4
    flip = one_hot_matrix(256, lambda r: 255 - r)
    per_chunk = chunk // block
    bands = parts[0].shape[1]
    count = halves // 2 * per_chunk

    def produce(t):
        s, b = t // per_chunk, t % per_chunk
        now = t % 2
        end = chunk - b * block
        near, back = [], []
        for c in range(2):
            mirror = parts[s ^ (halves - 1)]
            back.append(
                jnp.concatenate(
                    [
                        dot(mirror[1 - c, :, end - 256 * (i + 1) : end - 256 * i], flip)
                        for i in range(block // 256)
                    ],
                    axis=1,
                )
            )
            near.append(parts[s][c, :, b * block : (b + 1) * block].astype(F32))
        for v in range(NV):
            to = slice(v * NC, (v + 1) * NC)
            even = []
            for c in range(2):
                here = near[c][v : v + 1] * near[c][NV:bands]
                there = back[c][v : v + 1] * back[c][NV:bands]
                even.append(here + there)
                odds[now, to, c * block : (c + 1) * block] = (here - there).astype(BF16)
            evens[now, 0, to, :] = (even[0] + even[1]).astype(BF16)
            evens[now, 1, to, :] = (even[0] - even[1]).astype(BF16)

    def consume(t):
        now = t % 2
        for table_copy in table_copies[t : t + 1]:
            table_copy.wait()
        first, second, third = 3 * t * block, (3 * t + 1) * block, (3 * t + 3) * block
        terms = (
            dot(evens[now, 0], table[first:second, :quarter]),
            dot(evens[now, 1], table[first:second, quarter:]),
            dot(odds[now], table[second:third, :]),
        )
        for cols, term in zip((slice(0, quarter), slice(quarter, half), slice(half, waves)), terms):
            if t == 0:
                acc[:, cols] = term
            else:
                acc[:, cols] += term

    produce(0)
    for t in range(count):
        if t + 1 < count:
            produce(t + 1)
        consume(t)
    done = acc[...].astype(BF16)
    both = [
        jnp.concatenate([done[:, o : o + n] for o, n in pieces(waves, i, waves // 2)], axis=1)
        for i in range(2)
    ]
    if slot == 1:
        rho[...] = done
        order = interleave(waves // 2)
        natural_out[...] = jnp.concatenate([project(vec, part, order) for part in both], axis=1)
        copy.wait()
    else:
        rho_own[...] = jnp.where(x == 0, both[0], both[1])
        rho_msg[: NV * NC] = jnp.where(x == 0, both[1], both[0])
        rho_msg[NV * NC :] = pack(vec[...], rho_msg.shape[1])


def pack(array, width):
    rows, cols = array.shape
    if cols < width:
        step = rows * cols // width
        return jnp.concatenate([array[i : i + step] for i in range(0, rows, step)], axis=1)
    return jnp.concatenate([array[:, i : i + width] for i in range(0, cols, width)], axis=0)


def project(vec, rho, order):
    return dot(dot(vec[...], rho).astype(BF16), order).astype(BF16)


def back_kernel(*refs, shifts, rel):
    *vec, rho, screened = refs[: 3 - rel]
    outs = refs[3 - rel :]
    j, x = place(shifts)
    width = rho.shape[1]
    pair = 1 - x if rel else x
    products = rho[: NV * NC, :]
    if rel:
        vectors = pack(rho[NV * NC :, :], rho.shape[1] * (rho.shape[0] - NV * NC) // outs[0].shape[0])
    else:
        vectors = vec[0][...]
    first = dot(dot(vectors, products).astype(BF16), interleave(width)).astype(BF16)
    for s in range(shifts):
        for c in range(2):
            start = pl.multiple_of((c * shifts + (j ^ s)) * width, width)
            term = dot(first, screened[pair, :, pl.ds(start, width)])
            outs[s][:, c * width : (c + 1) * width] = term.astype(outs[s].dtype)


def cut(value, scratch, outs):
    shifts = len(outs)
    j = place(shifts)[0]
    scratch[...] = value.reshape(scratch.shape)
    for s in range(shifts):
        for c in range(2):
            outs[s][c] = scratch[c * shifts + (j ^ s)].astype(outs[s].dtype)


def forward_kernel(*refs, shifts):
    sources, refs = refs[: 2 * shifts], refs[2 * shifts :]
    rho_own, rho_far, screened = refs[:3]
    outs, scratch = refs[3:-1], refs[-1]
    j, x = place(shifts)
    width = rho_own.shape[1]
    order = interleave(width)
    for rel in range(2):
        pair = x if rel == 0 else 1 - x
        total = None
        for s in range(shifts):
            source = sources[rel * shifts + s]
            for c in range(2):
                start = pl.multiple_of((c * shifts + (j ^ s)) * width, width)
                term = dot_nt(
                    source[:, c * width : (c + 1) * width], screened[pair, :, pl.ds(start, width)]
                )
                total = term if total is None else total + term
        weight = dot_nt(total.astype(BF16), order).astype(BF16)
        products = (rho_far if rel else rho_own)[: NV * NC, :]
        cut(dot_nt(weight, products), scratch.at[rel], [out.at[rel] for out in outs])


def second_kernel(q_keep, q_far, *refs, shifts):
    received, rho = refs[: shifts - 1], refs[shifts - 1]
    others, outs, scratch = refs[shifts : 2 * shifts], refs[2 * shifts : -1], refs[-1]
    weight = q_keep[...] + q_far[...].astype(F32)
    for part in received:
        weight = weight + part[...].astype(F32)
    weight = weight.astype(BF16)
    waves = rho.shape[1]
    width = waves // 2
    order = interleave(width)
    parts = [
        dot_nt(weight[:, width * i : width * (i + 1)], order).astype(BF16) for i in range(2)
    ]
    cuts = (0, width // 4, width // 2, width)
    sorted_weight = jnp.concatenate(
        [p[:, lo:hi] for lo, hi in zip(cuts, cuts[1:]) for p in parts], axis=1
    )
    cut(dot_nt(sorted_weight, rho[...]), scratch, [out.at[2] for out in outs])
    for out, other in zip(outs, others):
        out[:2] = other[...]


def send_kernel(pairs, own, *refs, groups, halves):
    received, out = refs[:-1], refs[-1]
    parts = own.shape[1]
    x = place(halves)[1]
    first = lax.axis_index("pairs") * parts
    spots = ((0, first + x), (0, first + 1 - x), (1, first + x))
    owned = out.shape[1]
    total = own[...]
    for part in received:
        total = total + part[...].astype(F32)
    for k in range(groups * owned):
        for part in range(parts):
            value = jnp.zeros(own.shape[2:], F32)
            for term, (slot, index) in enumerate(spots):
                value = value + jnp.where(pairs[slot, index] == k, total[term, part], 0.0)
            out[k // owned * parts + part, k % owned] = value.astype(BF16)


def local(orbitals, vectors, screened, pair_list, band_order):
    groups = lax.axis_size("pairs")
    columns = lax.axis_size("pw")
    pairs_here = screened.shape[0]
    halves = columns // pairs_here
    both = ("pairs", "pw")
    w = lax.axis_index("pw")
    k_count, band_here, chunk = orbitals.shape
    points = chunk * columns
    waves = screened.shape[2]
    width = waves // columns
    own_waves = width * pairs_here
    transitions = vectors.shape[2]
    vec_count = vectors.shape[1] * groups
    vec_part = vectors.shape[1] // pairs_here
    bands = band_here * groups
    members = [
        [gg * columns + xx * halves + jj for gg in range(groups) for xx in range(pairs_here)]
        for jj in range(halves)
    ]

    def exchange(value):
        return lax.all_to_all(value, both, 0, 0, tiled=True, axis_index_groups=members)

    def shift(value, s):
        return lax.ppermute(value, "pw", [(i, i ^ s) for i in range(columns)])

    def call(kernel, outs, *args, flops=0, scratch=(), limit=4, far=0, cost=None):
        moved = cost or sum(math.prod(v.shape) * v.dtype.itemsize for v in (*args, *outs))
        return pl.pallas_call(
            kernel,
            in_specs=[vmem] * (len(args) - far) + [hbm] * far,
            out_specs=[vmem] * len(outs),
            out_shape=list(outs),
            scratch_shapes=list(scratch),
            compiler_params=pltpu.CompilerParams(vmem_limit_bytes=limit * 2**20),
            cost_estimate=pl.CostEstimate(flops=flops, bytes_accessed=moved, transcendentals=0),
        )(*args)

    smem = pl.BlockSpec(memory_space=pltpu.SMEM)
    vmem = pl.BlockSpec(memory_space=pltpu.VMEM)
    hbm = pl.BlockSpec(memory_space=pltpu.HBM)
    like = jax.ShapeDtypeStruct

    slots = 2 * groups * pairs_here
    sent = pl.pallas_call(
        functools.partial(gather_kernel, halves=halves),
        in_specs=[smem, hbm, hbm],
        out_specs=hbm,
        out_shape=like((slots // 2, 2, band_here, chunk + transitions), BF16),
        scratch_shapes=[
            pltpu.VMEM((slots // 2, 2, band_here, chunk + transitions), BF16),
            pltpu.VMEM(vectors.shape, BF16),
            pltpu.SemaphoreType.DMA((slots // 2, 2)),
            pltpu.SemaphoreType.DMA((slots // 2,)),
            pltpu.SemaphoreType.DMA,
        ],
        compiler_params=pltpu.CompilerParams(vmem_limit_bytes=60 * 2**20),
    )(pair_list.T, orbitals, vectors)
    got = exchange(sent).reshape(groups, pairs_here, 2, band_here, chunk + transitions)
    seeds = lax.dynamic_index_in_dim(
        jnp.asarray(phase_tables(points, waves, halves, columns)), w % halves, keepdims=False
    )
    vec = got[..., chunk:].transpose(2, 0, 1, 3, 4).reshape(2, vec_count, transitions)
    picker = (band_order[:, None] == jnp.arange(bands, dtype=jnp.int32)[None, :]).astype(BF16)
    half_waves = own_waves // 2
    block = min(2048, chunk)
    (table,) = call(
        functools.partial(table_kernel, block=block, chunk=chunk),
        [like((3 * points // 4, half_waves), BF16)],
        seeds,
        flops=3 * points * half_waves,
    )
    picker, table = lax.optimization_barrier((picker, table))
    psi = [
        jnp.einsum(
            "gbn,gxbr->xnr",
            picker.reshape(groups, band_here, bands),
            got[:, :, slot, :, :chunk],
            preferred_element_type=F32,
        ).astype(BF16)
        for slot in range(2)
    ]
    products = NV * NC

    def transform(slot, outs, *args):
        parts = [psi[slot]] + [shift(psi[slot], s) for s in range(1, halves)]
        return call(
            functools.partial(transform_kernel, halves=halves, slot=slot),
            outs,
            *parts,
            *args,
            flops=products * points * own_waves,
            scratch=[
                pltpu.VMEM((2, 2, products, block), BF16),
                pltpu.VMEM((2, products, 2 * block), BF16),
                pltpu.VMEM((products, own_waves), F32),
            ]
            + [pltpu.SemaphoreType.DMA if slot else pltpu.SemaphoreType.DMA((points // 4 // block,))],
            limit=24 if slot else 36,
            far=1,
        )

    part = like((products, width), BF16)
    packed = like((products + vec_count * transitions // width, width), BF16)
    rho_own, rho_msg, table = transform(0, [part, packed, like(table.shape, BF16)], vec[0], table)
    rho_far = shift(rho_msg, halves)
    full = like((vec_count, own_waves), BF16)
    rho, p_second, screened = transform(
        1,
        [like((products, own_waves), BF16), full, like(screened.shape, BF16)],
        vec[1],
        table,
        screened,
    )

    rho_own, p_second = lax.optimization_barrier((rho_own, p_second))
    far = shift(p_second, halves)
    near = [shift(p_second, s) for s in range(1, halves)]
    fars = [shift(far, s) for s in range(1, halves)]
    flops = 4 * vec_count * width * waves
    partial_q = like((vec_count, own_waves), F32)
    q_outs = [partial_q] + [like((vec_count, own_waves), BF16)] * (halves - 1)
    q_keep, *q_near = call(
        functools.partial(back_kernel, shifts=halves, rel=0),
        q_outs,
        vec[0],
        rho_own,
        screened,
        cost=1,
    )
    rho_far, q_keep = lax.optimization_barrier((rho_far, q_keep))
    q_part, *q_msgs = call(
        functools.partial(back_kernel, shifts=halves, rel=1),
        q_outs,
        rho_far,
        screened,
        cost=1,
    )
    received = [[shift(v, s + 1) for s, v in enumerate(part)] for part in (q_near, q_msgs)]
    q_send = (q_part + sum(v.astype(F32) for v in received[1])).astype(BF16)
    q_far = shift(q_send, halves)
    vec_rows = vec_count // columns
    shape = (pairs_here, vec_rows, transitions)
    forward = call(
        functools.partial(forward_kernel, shifts=halves),
        [like((2, *shape), F32)] + [like((2, *shape), BF16)] * (halves - 1),
        p_second,
        *near,
        far,
        *fars,
        rho_own,
        rho_far,
        screened,
        cost=1,
        scratch=[pltpu.VMEM((2, columns, vec_rows, transitions), F32)],
    )
    out_own, *out_msgs = call(
        functools.partial(second_kernel, shifts=halves),
        [like((3, *shape), F32)] + [like((3, *shape), BF16)] * (halves - 1),
        q_keep,
        q_far,
        *received[0],
        rho,
        *forward,
        flops=2 * vec_count * products * own_waves,
        scratch=[pltpu.VMEM((columns, vec_rows, transitions), F32)],
    )

    received = [shift(out_msgs[s - 1], s) for s in range(1, halves)]
    placed = pl.pallas_call(
        functools.partial(send_kernel, groups=groups, halves=halves),
        in_specs=[smem] + [vmem] * halves,
        out_specs=vmem,
        out_shape=like(
            (groups * pairs_here, k_count // groups, vec_rows, transitions), BF16
        ),
        compiler_params=pltpu.CompilerParams(vmem_limit_bytes=4 * 2**20),
    )(pair_list.T, out_own, *received)
    return jnp.sum(exchange(placed).astype(F32), axis=0)


def solution(mesh):
    in_specs = (P(None, "pairs", "pw"), P(None, "pairs", None), P("pairs", "pw", None), P(), P())
    out_specs = P("pairs", "pw", None)
    return jax.shard_map(local, mesh=mesh, in_specs=in_specs, out_specs=out_specs, check_vma=False)
```

```python
import functools
import math

import jax
import jax.numpy as jnp
import numpy as np
from jax import lax
from jax.experimental import pallas as pl
from jax.experimental.pallas import tpu as pltpu
from jax.sharding import PartitionSpec as P

NV = 16
NC = 16
FINE = 64
BF16 = jnp.bfloat16
F32 = jnp.float32


def column_order(size):
    return np.concatenate([np.arange(0, size, 4), np.arange(2, size, 4), np.arange(1, size, 2)])


def phase_tables(points, waves, halves, columns):
    width, chunk = waves // columns, points // columns
    period, turn = 4 * points, math.pi / (2 * points)
    scale = math.sqrt(2.0 / points)
    seeds = []
    for j in range(halves):
        own = np.concatenate(
            [np.arange(c * width, (c + 1) * width) for c in range(j, columns, halves)]
        )
        own = own[column_order(own.size)].astype(np.int64)
        starts = np.concatenate(
            [
                np.arange((c * halves + (j ^ s)) * chunk, (c * halves + (j ^ s) + 1) * chunk, FINE)
                for s in range(halves // 2)
                for c in range(columns // halves)
            ]
        )
        coarse = (2 * starts[:, None] * own) % period * turn
        fine = ((2 * np.arange(FINE) + 1)[:, None] * own) % period * turn
        seeds.append(
            [
                np.concatenate([np.cos(coarse) * scale, np.cos(fine)]),
                np.concatenate([np.sin(coarse) * scale, np.sin(fine)]),
            ]
        )
    return np.array(seeds).astype(np.float32)


def one_hot_matrix(size, target):
    rows = lax.broadcasted_iota(jnp.int32, (size, size), 0)
    cols = lax.broadcasted_iota(jnp.int32, (size, size), 1)
    return jnp.where(target(rows) == cols, 1.0, 0.0).astype(BF16)


def interleave(size):
    part = size // 4
    return one_hot_matrix(
        size,
        lambda r: jnp.where(r < part, 4 * r, jnp.where(r < 2 * part, 4 * r - size + 2, 2 * r - size + 1)),
    )


def pieces(waves, i, size):
    part, quarter = size // 4, waves // 4
    yield i * part, part
    yield quarter + i * part, part
    yield 2 * quarter + 2 * i * part, 2 * part


def place(halves):
    w = lax.axis_index("pw")
    return lax.rem(w, halves), lax.div(w, halves)


def dot(a, b):
    return jnp.dot(a, b, preferred_element_type=F32)


def dot_nt(a, b):
    return lax.dot_general(a, b, (((1,), (1,)), ((), ())), preferred_element_type=F32)


def gather_kernel(
    requests, orbitals, far_vectors, out, held, vectors, load, store, fetch, *, halves
):
    count, slots, rows = out.shape[:3]
    chunk = orbitals.shape[2]
    fetched = pltpu.make_async_copy(far_vectors, vectors, fetch)
    fetched.start()

    def load_of(i, slot):
        return pltpu.make_async_copy(
            orbitals.at[requests[slot, i]], held.at[i, slot, :, pl.ds(0, chunk)], load.at[i, slot]
        )

    def start(i, carry):
        for slot in range(slots):
            load_of(i, slot).start()
        return carry

    lax.fori_loop(0, count, start, 0)
    x = place(halves)[1]
    fetched.wait()

    def pick(i, carry):
        for slot in range(slots):
            block = vectors[requests[slot, i]]
            held[i, slot, :, chunk:] = jnp.where(x == 0, block[:rows], block[rows:])
        return carry

    lax.fori_loop(0, count, pick, 0)

    def send(i, carry):
        for slot in range(slots):
            load_of(i, slot).wait()
        pltpu.make_async_copy(held.at[i], out.at[i], store.at[i]).start()
        return carry

    lax.fori_loop(0, count, send, 0)

    def end(i, carry):
        pltpu.make_async_copy(held.at[i], out.at[i], store.at[i]).wait()
        return carry

    lax.fori_loop(0, count, end, 0)


def table_kernel(seeds, table, *, block, chunk):
    half = table.shape[1]
    coarse = seeds.shape[1] - FINE
    per_chunk, rows = chunk // block, block // FINE
    for c in range(2):
        cols = slice(0, 2 * half) if c == 0 else slice(half, 2 * half)
        cb, sb = seeds[0, coarse:, cols], seeds[1, coarse:, cols]
        for t in range(table.shape[0] // (3 * block)):
            s, b = t // per_chunk, t % per_chunk

            def step(a, carry):
                row = (s * 2 + c) * per_chunk * rows + b * rows + a
                ca, sa = seeds[0, pl.ds(row, 1), :], seeds[1, pl.ds(row, 1), :]
                fresh = (ca[:, cols] * cb - sa[:, cols] * sb).astype(BF16)
                to = pl.multiple_of(3 * t * block + a * FINE, FINE)
                if c == 0:
                    table[pl.ds(to, FINE), :] = fresh[:, :half]
                    fresh = fresh[:, half:]
                to = pl.multiple_of((3 * t + 1 + c) * block + a * FINE, FINE)
                table[pl.ds(to, FINE), :] = fresh
                return carry

            lax.fori_loop(0, rows, step, 0, unroll=2)


def transform_kernel(*refs, halves, slot):
    parts, refs = refs[:halves], refs[halves:]
    table_copies = []
    if slot == 0:
        vec, far_table, rho_own, rho_msg, table, sem = *refs[:5], refs[-1]
        for i in range(3 * sem.shape[0]):
            size = table.shape[0] // (3 * sem.shape[0])
            span = pl.ds(i * size, size)
            table_copies.append(
                pltpu.make_async_copy(far_table.at[span], table.at[span], sem.at[i // 3, i % 3])
            )
            table_copies[-1].start()
    else:
        vec, table, far_screened, rho, natural_out, screened = refs[:6]
        copy = pltpu.make_async_copy(far_screened, screened, refs[-1])
        copy.start()
    refs = refs[:-1]
    evens, odds, acc = refs[-3:]
    x = place(halves)[1]
    chunk = parts[0].shape[2]
    block = evens.shape[3]
    waves = acc.shape[1]
    half, quarter = waves // 2, waves // 4
    flip = one_hot_matrix(256, lambda r: 255 - r)
    per_chunk = chunk // block
    bands = parts[0].shape[1]
    count = halves // 2 * per_chunk

    def produce(t):
        s, b = t // per_chunk, t % per_chunk
        now = t % 2
        end = chunk - b * block
        near, back = [], []
        for c in range(2):
            mirror = parts[s ^ (halves - 1)]
            back.append(
                jnp.concatenate(
                    [
                        dot(mirror[1 - c, :, end - 256 * (i + 1) : end - 256 * i], flip)
                        for i in range(block // 256)
                    ],
                    axis=1,
                )
            )
            near.append(parts[s][c, :, b * block : (b + 1) * block].astype(F32))
        for v in range(NV):
            to = slice(v * NC, (v + 1) * NC)
            even = []
            for c in range(2):
                here = near[c][v : v + 1] * near[c][NV:bands]
                there = back[c][v : v + 1] * back[c][NV:bands]
                even.append(here + there)
                odds[now, to, c * block : (c + 1) * block] = (here - there).astype(BF16)
            evens[now, 0, to, :] = (even[0] + even[1]).astype(BF16)
            evens[now, 1, to, :] = (even[0] - even[1]).astype(BF16)

    def consume(t):
        now = t % 2
        first, second, third = 3 * t * block, (3 * t + 1) * block, (3 * t + 3) * block
        for table_copy in table_copies[3 * t : 3 * t + 1]:
            table_copy.wait()
        terms = [
            dot(evens[now, 0], table[first:second, :quarter]),
            dot(evens[now, 1], table[first:second, quarter:]),
        ]
        for table_copy in table_copies[3 * t + 1 : 3 * t + 3]:
            table_copy.wait()
        terms.append(dot(odds[now], table[second:third, :]))
        for cols, term in zip((slice(0, quarter), slice(quarter, half), slice(half, waves)), terms):
            if t == 0:
                acc[:, cols] = term
            else:
                acc[:, cols] += term

    produce(0)
    for t in range(count):
        if t + 1 < count:
            produce(t + 1)
        consume(t)
    done = acc[...].astype(BF16)
    both = [
        jnp.concatenate([done[:, o : o + n] for o, n in pieces(waves, i, waves // 2)], axis=1)
        for i in range(2)
    ]
    if slot == 1:
        rho[...] = done
        order = interleave(waves // 2)
        natural_out[...] = jnp.concatenate([project(vec, part, order) for part in both], axis=1)
        copy.wait()
    else:
        rho_own[...] = jnp.where(x == 0, both[0], both[1])
        rho_msg[: NV * NC] = jnp.where(x == 0, both[1], both[0])
        rho_msg[NV * NC :] = pack(vec[...], rho_msg.shape[1])


def pack(array, width):
    rows, cols = array.shape
    if cols < width:
        step = rows * cols // width
        return jnp.concatenate([array[i : i + step] for i in range(0, rows, step)], axis=1)
    return jnp.concatenate([array[:, i : i + width] for i in range(0, cols, width)], axis=0)


def project(vec, rho, order):
    return dot(dot(vec[...], rho).astype(BF16), order).astype(BF16)


def back_kernel(*refs, shifts, rel):
    *vec, rho, screened = refs[: 3 - rel]
    outs = refs[3 - rel :]
    j, x = place(shifts)
    width = rho.shape[1]
    pair = 1 - x if rel else x
    products = rho[: NV * NC, :]
    if rel:
        vectors = pack(rho[NV * NC :, :], rho.shape[1] * (rho.shape[0] - NV * NC) // outs[0].shape[0])
    else:
        vectors = vec[0][...]
    first = dot(dot(vectors, products).astype(BF16), interleave(width)).astype(BF16)
    for s in range(shifts):
        for c in range(2):
            start = pl.multiple_of((c * shifts + (j ^ s)) * width, width)
            term = dot(first, screened[pair, :, pl.ds(start, width)])
            outs[s][:, c * width : (c + 1) * width] = term.astype(outs[s].dtype)


def cut(value, scratch, outs):
    shifts = len(outs)
    j = place(shifts)[0]
    scratch[...] = value.reshape(scratch.shape)
    for s in range(shifts):
        for c in range(2):
            outs[s][c] = scratch[c * shifts + (j ^ s)].astype(outs[s].dtype)


def forward_kernel(*refs, shifts):
    sources, refs = refs[: 2 * shifts], refs[2 * shifts :]
    rho_own, rho_far, screened = refs[:3]
    outs, scratch = refs[3:-1], refs[-1]
    j, x = place(shifts)
    width = rho_own.shape[1]
    order = interleave(width)
    for rel in range(2):
        pair = x if rel == 0 else 1 - x
        total = None
        for s in range(shifts):
            source = sources[rel * shifts + s]
            for c in range(2):
                start = pl.multiple_of((c * shifts + (j ^ s)) * width, width)
                term = dot_nt(
                    source[:, c * width : (c + 1) * width], screened[pair, :, pl.ds(start, width)]
                )
                total = term if total is None else total + term
        weight = dot_nt(total.astype(BF16), order).astype(BF16)
        products = (rho_far if rel else rho_own)[: NV * NC, :]
        cut(dot_nt(weight, products), scratch.at[rel], [out.at[rel] for out in outs])


def second_kernel(q_keep, q_far, *refs, shifts):
    received, rho = refs[: shifts - 1], refs[shifts - 1]
    others, outs, scratch = refs[shifts : 2 * shifts], refs[2 * shifts : -1], refs[-1]
    weight = q_keep[...] + q_far[...].astype(F32)
    for part in received:
        weight = weight + part[...].astype(F32)
    weight = weight.astype(BF16)
    waves = rho.shape[1]
    width = waves // 2
    order = interleave(width)
    parts = [
        dot_nt(weight[:, width * i : width * (i + 1)], order).astype(BF16) for i in range(2)
    ]
    cuts = (0, width // 4, width // 2, width)
    sorted_weight = jnp.concatenate(
        [p[:, lo:hi] for lo, hi in zip(cuts, cuts[1:]) for p in parts], axis=1
    )
    cut(dot_nt(sorted_weight, rho[...]), scratch, [out.at[2] for out in outs])
    for out, other in zip(outs, others):
        out[:2] = other[...]


def send_kernel(pairs, own, *refs, groups, halves):
    received, out = refs[:-1], refs[-1]
    parts = own.shape[1]
    x = place(halves)[1]
    first = lax.axis_index("pairs") * parts
    spots = ((0, first + x), (0, first + 1 - x), (1, first + x))
    owned = out.shape[1]
    total = own[...]
    for part in received:
        total = total + part[...].astype(F32)
    for k in range(groups * owned):
        for part in range(parts):
            value = jnp.zeros(own.shape[2:], F32)
            for term, (slot, index) in enumerate(spots):
                value = value + jnp.where(pairs[slot, index] == k, total[term, part], 0.0)
            out[k // owned * parts + part, k % owned] = value.astype(BF16)


def local(orbitals, vectors, screened, pair_list, band_order):
    groups = lax.axis_size("pairs")
    columns = lax.axis_size("pw")
    pairs_here = screened.shape[0]
    halves = columns // pairs_here
    both = ("pairs", "pw")
    w = lax.axis_index("pw")
    k_count, band_here, chunk = orbitals.shape
    points = chunk * columns
    waves = screened.shape[2]
    width = waves // columns
    own_waves = width * pairs_here
    transitions = vectors.shape[2]
    vec_count = vectors.shape[1] * groups
    vec_part = vectors.shape[1] // pairs_here
    bands = band_here * groups
    members = [
        [gg * columns + xx * halves + jj for gg in range(groups) for xx in range(pairs_here)]
        for jj in range(halves)
    ]

    def exchange(value):
        return lax.all_to_all(value, both, 0, 0, tiled=True, axis_index_groups=members)

    def shift(value, s):
        return lax.ppermute(value, "pw", [(i, i ^ s) for i in range(columns)])

    def call(kernel, outs, *args, flops=0, scratch=(), limit=4, far=0, cost=None):
        moved = cost or sum(math.prod(v.shape) * v.dtype.itemsize for v in (*args, *outs))
        return pl.pallas_call(
            kernel,
            in_specs=[vmem] * (len(args) - far) + [hbm] * far,
            out_specs=[vmem] * len(outs),
            out_shape=list(outs),
            scratch_shapes=list(scratch),
            compiler_params=pltpu.CompilerParams(vmem_limit_bytes=limit * 2**20),
            cost_estimate=pl.CostEstimate(flops=flops, bytes_accessed=moved, transcendentals=0),
        )(*args)

    smem = pl.BlockSpec(memory_space=pltpu.SMEM)
    vmem = pl.BlockSpec(memory_space=pltpu.VMEM)
    hbm = pl.BlockSpec(memory_space=pltpu.HBM)
    like = jax.ShapeDtypeStruct

    slots = 2 * groups * pairs_here
    sent = pl.pallas_call(
        functools.partial(gather_kernel, halves=halves),
        in_specs=[smem, hbm, hbm],
        out_specs=hbm,
        out_shape=like((slots // 2, 2, band_here, chunk + transitions), BF16),
        scratch_shapes=[
            pltpu.VMEM((slots // 2, 2, band_here, chunk + transitions), BF16),
            pltpu.VMEM(vectors.shape, BF16),
            pltpu.SemaphoreType.DMA((slots // 2, 2)),
            pltpu.SemaphoreType.DMA((slots // 2,)),
            pltpu.SemaphoreType.DMA,
        ],
        compiler_params=pltpu.CompilerParams(vmem_limit_bytes=60 * 2**20),
    )(pair_list.T, orbitals, vectors)
    got = exchange(sent).reshape(groups, pairs_here, 2, band_here, chunk + transitions)
    seeds = lax.dynamic_index_in_dim(
        jnp.asarray(phase_tables(points, waves, halves, columns)), w % halves, keepdims=False
    )
    vec = got[..., chunk:].transpose(2, 0, 1, 3, 4).reshape(2, vec_count, transitions)
    picker = (band_order[:, None] == jnp.arange(bands, dtype=jnp.int32)[None, :]).astype(BF16)
    half_waves = own_waves // 2
    block = min(2048, chunk)
    (table,) = call(
        functools.partial(table_kernel, block=block, chunk=chunk),
        [like((3 * points // 4, half_waves), BF16)],
        seeds,
        flops=3 * points * half_waves,
    )
    picker, table = lax.optimization_barrier((picker, table))
    psi = [
        jnp.einsum(
            "gbn,gxbr->xnr",
            picker.reshape(groups, band_here, bands),
            got[:, :, slot, :, :chunk],
            preferred_element_type=F32,
        ).astype(BF16)
        for slot in range(2)
    ]
    products = NV * NC

    def transform(slot, outs, *args):
        parts = [psi[slot]] + [shift(psi[slot], s) for s in range(1, halves)]
        return call(
            functools.partial(transform_kernel, halves=halves, slot=slot),
            outs,
            *parts,
            *args,
            flops=products * points * own_waves,
            scratch=[
                pltpu.VMEM((2, 2, products, block), BF16),
                pltpu.VMEM((2, products, 2 * block), BF16),
                pltpu.VMEM((products, own_waves), F32),
            ]
            + [pltpu.SemaphoreType.DMA if slot else pltpu.SemaphoreType.DMA((points // 4 // block, 3))],
            limit=24 if slot else 36,
            far=1,
        )

    part = like((products, width), BF16)
    packed = like((products + vec_count * transitions // width, width), BF16)
    rho_own, rho_msg, table = transform(0, [part, packed, like(table.shape, BF16)], vec[0], table)
    rho_far = shift(rho_msg, halves)
    full = like((vec_count, own_waves), BF16)
    rho, p_second, screened = transform(
        1,
        [like((products, own_waves), BF16), full, like(screened.shape, BF16)],
        vec[1],
        table,
        screened,
    )

    rho_own, p_second = lax.optimization_barrier((rho_own, p_second))
    far = shift(p_second, halves)
    near = [shift(p_second, s) for s in range(1, halves)]
    fars = [shift(far, s) for s in range(1, halves)]
    flops = 4 * vec_count * width * waves
    partial_q = like((vec_count, own_waves), F32)
    q_outs = [partial_q] + [like((vec_count, own_waves), BF16)] * (halves - 1)
    q_keep, *q_near = call(
        functools.partial(back_kernel, shifts=halves, rel=0),
        q_outs,
        vec[0],
        rho_own,
        screened,
        cost=1,
    )
    rho_far, q_keep = lax.optimization_barrier((rho_far, q_keep))
    q_part, *q_msgs = call(
        functools.partial(back_kernel, shifts=halves, rel=1),
        q_outs,
        rho_far,
        screened,
        cost=1,
    )
    received = [[shift(v, s + 1) for s, v in enumerate(part)] for part in (q_near, q_msgs)]
    q_send = (q_part + sum(v.astype(F32) for v in received[1])).astype(BF16)
    q_far = shift(q_send, halves)
    vec_rows = vec_count // columns
    shape = (pairs_here, vec_rows, transitions)
    forward = call(
        functools.partial(forward_kernel, shifts=halves),
        [like((2, *shape), F32)] + [like((2, *shape), BF16)] * (halves - 1),
        p_second,
        *near,
        far,
        *fars,
        rho_own,
        rho_far,
        screened,
        cost=1,
        scratch=[pltpu.VMEM((2, columns, vec_rows, transitions), F32)],
    )
    out_own, *out_msgs = call(
        functools.partial(second_kernel, shifts=halves),
        [like((3, *shape), F32)] + [like((3, *shape), BF16)] * (halves - 1),
        q_keep,
        q_far,
        *received[0],
        rho,
        *forward,
        flops=2 * vec_count * products * own_waves,
        scratch=[pltpu.VMEM((columns, vec_rows, transitions), F32)],
    )

    received = [shift(out_msgs[s - 1], s) for s in range(1, halves)]
    placed = pl.pallas_call(
        functools.partial(send_kernel, groups=groups, halves=halves),
        in_specs=[smem] + [vmem] * halves,
        out_specs=vmem,
        out_shape=like(
            (groups * pairs_here, k_count // groups, vec_rows, transitions), BF16
        ),
        compiler_params=pltpu.CompilerParams(vmem_limit_bytes=4 * 2**20),
    )(pair_list.T, out_own, *received)
    return jnp.sum(exchange(placed).astype(F32), axis=0)


def solution(mesh):
    in_specs = (P(None, "pairs", "pw"), P(None, "pairs", None), P("pairs", "pw", None), P(), P())
    out_specs = P("pairs", "pw", None)
    return jax.shard_map(local, mesh=mesh, in_specs=in_specs, out_specs=out_specs, check_vma=False)
```
